256 devices in a mesh: ctx: 32 (over z, x), head: 8 (over y, core).
Axes of the slice: x: 4, y: 4, z: 8, core: 2. Of those that a mesh axis runs over, the one named last changes fastest.
Arguments:
- queries: bfloat16 [65536, 4096], P(('ctx', 'head')), may hold values from -8 to 8
- new_keys: bfloat16 [65536, 1024], P(('ctx', 'head')), may hold values from -4 to 4
- new_values: bfloat16 [65536, 1024], P(('ctx', 'head')), may hold values from -4 to 4
- cache_keys: bfloat16 [131072, 1024], P('ctx', 'head'), may hold values from -4 to 4
- cache_values: bfloat16 [131072, 1024], P('ctx', 'head'), may hold values from -4 to 4
- chosen: int32 [128, 8, 3], P('ctx', 'head'), may hold values from 0 to 255, as said below
Outputs:
- attended: bfloat16 [65536, 4096], P(('ctx', 'head'))
The draws below stay inside these ranges and needn't reach their ends.
Inputs may be any that keep to these rules, and one draw needn't show every extreme that they name: `chosen`: for each query block and key-value head the 3 ids are distinct. Cache block j lies on the device of index j // 8 along ctx. For each key-value head, the 4 query blocks of one device along ctx name the blocks of any one device at most 1 times together, and those of some device exactly 1 times.
All inputs are finite; a program needn't handle non-finite values.
Results may differ from the reference program's by a relative error of at most 0.0048.
Values may be sent and summed in bfloat16 or wider, within the bound.
No kernel may reach another device: no remote copies, remote signals or barrier semaphores. Data moves between devices by JAX's collectives and lax.ppermute only.
A program may use at most 192 MiB of HBM per device.

```python
import math
import jax
import jax.numpy as jnp
from jax import lax

HQ = 32
KVH = 8
HD = 128
BLK = 512
TOPK = 3
QB_DEV = 4
GROUP = 4
CB_DEV = 8
MOST = 1
QBLOCKS = 128
KBLOCKS = 256
TOKENS = 65536
CTXTOK = 131072


def draw_queries(key, part):
    key = jax.random.fold_in(key, 3)
    base = jax.random.truncated_normal(key, -4.0, 4.0, (TOKENS, HQ * HD), jnp.float32)
    return base.astype(jnp.bfloat16)


def draw_new_keys(key, part):
    key = jax.random.fold_in(key, 5)
    base = jax.random.truncated_normal(key, -4.0, 4.0, (TOKENS, KVH * HD), jnp.float32)
    return base.astype(jnp.bfloat16)


def draw_chosen(key, part):
    key = jax.random.fold_in(key, 11)
    devices_ctx = KBLOCKS // CB_DEV
    slot_count = QB_DEV * TOPK
    group_count = (slot_count + MOST - 1) // MOST

    def draw_single(subkey):
        first_key, second_key, third_key = jax.random.split(subkey, 3)
        ordering = jax.random.permutation(first_key, slot_count)
        owner_ids = jax.random.permutation(second_key, devices_ctx)[:group_count]
        slot_index = jnp.arange(slot_count)
        group_of = slot_index // MOST
        place_in = slot_index % MOST
        local_perm = jax.vmap(lambda inner: jax.random.permutation(inner, CB_DEV))(jax.random.split(third_key, group_count))
        block_ids = owner_ids[group_of] * CB_DEV + local_perm[group_of, place_in]
        placed = jnp.zeros((slot_count,), jnp.int32).at[ordering].set(block_ids.astype(jnp.int32))
        return placed.reshape(QB_DEV, TOPK)
    subkeys = jax.random.split(key, devices_ctx * KVH)
    drawn_ids = jax.vmap(draw_single)(subkeys).reshape(devices_ctx, KVH, QB_DEV, TOPK)
    return drawn_ids.transpose(0, 2, 1, 3).reshape(devices_ctx * QB_DEV, KVH, TOPK)


def block_levels(key, dims, shards, low, largest):
    level = 1.0
    for axis_at, parts in shards:
        heights = jax.random.uniform(jax.random.fold_in(jax.random.fold_in(key, 6), axis_at), (parts,), jnp.float32, low / len(shards), largest / len(shards))
        level = level * jnp.repeat(jnp.exp(heights), dims[axis_at] // parts).reshape((-1,) + (1,) * (len(dims) - 1 - axis_at))
    return level


def bell_draw(stream_key, extent, spread, bound, shards=(), dtype=jnp.bfloat16):
    factor_of = block_levels(stream_key, extent, shards, -0.22, 0.18) if shards else 1.0
    entries = jax.random.normal(stream_key, extent, jnp.float32) * spread * factor_of
    return jnp.minimum(jnp.maximum(entries, -bound), bound).astype(dtype)


def setup_inputs(seed: int = 0) -> dict:
    keys = jax.random.split(jax.random.key(seed), 7)
    return {
        "queries": draw_queries(jax.random.fold_in(keys[6], 71), 0),
        "new_keys": draw_new_keys(jax.random.fold_in(keys[6], 71), 0),
        "new_values": bell_draw(keys[2], (TOKENS, KVH * HD), 1.0, 4.0, ((0, 256),)),
        "cache_keys": bell_draw(keys[3], (CTXTOK, KVH * HD), 1.0, 4.0, ((0, 32), (1, 8))),
        "cache_values": bell_draw(keys[4], (CTXTOK, KVH * HD), 1.0, 4.0, ((0, 32), (1, 8))),
        "chosen": draw_chosen(jax.random.fold_in(keys[6], 71), 0),
    }


def reference(queries, new_keys, new_values, cache_keys, cache_values, chosen):
    score_scale = 1.0 / math.sqrt(HD)
    query_grid = queries.reshape(QBLOCKS, BLK, KVH, GROUP, HD)
    keys_new = new_keys.reshape(QBLOCKS, BLK, KVH, HD)
    values_new = new_values.reshape(QBLOCKS, BLK, KVH, HD)
    cache_k = cache_keys.reshape(KBLOCKS, BLK, KVH, HD).transpose(2, 0, 1, 3)
    cache_v = cache_values.reshape(KBLOCKS, BLK, KVH, HD).transpose(2, 0, 1, 3)
    head_index = jnp.arange(KVH)[:, None]
    causal = jnp.arange(BLK)[None, :] <= jnp.arange(BLK)[:, None]
    visible = jnp.concatenate([jnp.ones((BLK, TOPK * BLK), bool), causal], axis=1)

    def one_block(packed):
        query_rows, own_keys, own_values, picked = packed
        far_keys = cache_k[head_index, picked].reshape(KVH, TOPK * BLK, HD)
        far_values = cache_v[head_index, picked].reshape(KVH, TOPK * BLK, HD)
        all_keys = jnp.concatenate([far_keys, own_keys.transpose(1, 0, 2)], axis=1)
        all_values = jnp.concatenate([far_values, own_values.transpose(1, 0, 2)], axis=1)
        scores = jnp.einsum('tkgd,ksd->kgts', query_rows.astype(jnp.float32), all_keys.astype(jnp.float32)) * score_scale
        scores = jnp.where(visible, scores, -jnp.inf)
        row_max = lax.optimization_barrier(jnp.max(scores, axis=3, keepdims=True))
        weights = jnp.exp(scores - row_max)
        totals = lax.optimization_barrier(jnp.sum(weights, axis=3, keepdims=True))
        weights_bf = weights.astype(jnp.bfloat16)
        mixed_out = jnp.einsum('kgts,ksd->tkgd', weights_bf.astype(jnp.float32), all_values.astype(jnp.float32))
        mixed_out = mixed_out / totals.transpose(2, 0, 1, 3)
        return mixed_out.astype(jnp.bfloat16).reshape(BLK, KVH * GROUP * HD)
    blocks_out = lax.map(one_block, (query_grid, keys_new, values_new, chosen))
    return blocks_out.reshape(TOKENS, HQ * HD)
```

```python
import functools
import math

import jax
import jax.numpy as jnp
from jax import lax
from jax.experimental import pallas as pl
from jax.experimental.pallas import tpu as pltpu
from jax.sharding import Mesh
from jax.sharding import PartitionSpec as P

HD = 128
BLK = 512
EXP_SCALE = math.log2(math.e) / math.sqrt(HD)
NEG = -1e30
NT = (((1,), (1,)), ((), ()))
NN = (((1,), (0,)), ((), ()))


def spread_kernel(k_ref, v_ref, o_ref):
    o_ref[:, 0] = jnp.swapaxes(k_ref[...], 0, 1)
    o_ref[:, 1] = jnp.swapaxes(v_ref[...], 0, 1)


def spread(cache_keys, cache_values, pieces):
    blocks = cache_keys.shape[0] // BLK
    rows = BLK // pieces
    step = 8
    shape = (blocks, pieces, rows, HD)
    block = pl.BlockSpec((blocks, step, rows, HD), lambda i: (0, i, 0, 0))
    return pl.pallas_call(
        spread_kernel,
        grid=(pieces // step,),
        in_specs=[block, block],
        out_specs=pl.BlockSpec((step, 2, blocks, rows, HD), lambda i: (i, 0, 0, 0, 0)),
        out_shape=jax.ShapeDtypeStruct((pieces, 2, blocks, rows, HD), cache_keys.dtype),
        name="spread",
    )(cache_keys.reshape(shape), cache_values.reshape(shape))


def pick_kernel(ids_ref, held_ref, o_ref, *, step, picks, blocks):
    first = pl.program_id(0) * step

    def one(i, carry):
        for j in range(picks):
            block_id = ids_ref[(first + i) * picks + j]
            src = block_id // blocks
            at = block_id % blocks
            o_ref[i, 0, j] = held_ref[src, 0, at]
            o_ref[i, 1, j] = held_ref[src, 1, at]
        return carry

    lax.fori_loop(0, step, one, 0, unroll=4)


def pick(ids, held, picks):
    sources, _, blocks, rows, _ = held.shape
    query_blocks = ids.shape[0] // picks
    step = 16
    return pl.pallas_call(
        functools.partial(pick_kernel, step=step, picks=picks, blocks=blocks),
        grid_spec=pltpu.PrefetchScalarGridSpec(
            num_scalar_prefetch=1,
            grid=(query_blocks // step,),
            in_specs=[pl.BlockSpec(held.shape, lambda i, ids: (0, 0, 0, 0, 0))],
            out_specs=pl.BlockSpec((step, 2, picks, rows, HD), lambda i, ids: (i, 0, 0, 0, 0)),
        ),
        out_shape=jax.ShapeDtypeStruct((query_blocks, 2, picks, rows, HD), held.dtype),
        name="pick",
    )(ids, held)


def near_kernel(core_ref, q_ref, k_ref, v_ref, acc_ref, stat_ref, *, group):
    rows = q_ref.shape[0]
    keys = k_ref[...]
    values = v_ref[...]
    q_at = core_ref[0] * rows + lax.broadcasted_iota(jnp.int32, (rows, BLK), 0)
    seen = lax.broadcasted_iota(jnp.int32, (rows, BLK), 1) <= q_at
    for g in range(group):
        cols = slice(g * HD, (g + 1) * HD)
        raw = lax.dot_general(q_ref[:, cols], keys, NT, preferred_element_type=jnp.float32)
        raw = jnp.where(seen, raw, NEG)
        top = jnp.max(raw, axis=1, keepdims=True)
        weights = jnp.where(seen, jnp.exp2((raw - top) * EXP_SCALE), 0.0)
        total = jnp.sum(weights, axis=1, keepdims=True)
        acc_ref[:, cols] = lax.dot_general(
            weights.astype(jnp.bfloat16), values, NN, preferred_element_type=jnp.float32
        )
        stat_ref[0, :, 2 * g : 2 * g + 1] = top
        stat_ref[0, :, 2 * g + 1 : 2 * g + 2] = total


def near_part(core, queries, keys, values):
    rows, width = queries.shape
    heads = keys.shape[1] // HD
    group = width // (heads * HD)
    return pl.pallas_call(
        functools.partial(near_kernel, group=group),
        grid_spec=pltpu.PrefetchScalarGridSpec(
            num_scalar_prefetch=1,
            grid=(heads,),
            in_specs=[
                pl.BlockSpec((rows, group * HD), lambda h, core: (0, h)),
                pl.BlockSpec((BLK, HD), lambda h, core: (0, h)),
                pl.BlockSpec((BLK, HD), lambda h, core: (0, h)),
            ],
            out_specs=[
                pl.BlockSpec((rows, group * HD), lambda h, core: (0, h)),
                pl.BlockSpec((1, rows, 2 * group), lambda h, core: (h, 0, 0)),
            ],
        ),
        out_shape=[
            jax.ShapeDtypeStruct((rows, width), jnp.float32),
            jax.ShapeDtypeStruct((heads, rows, 2 * group), jnp.float32),
        ],
        cost_estimate=pl.CostEstimate(
            flops=4 * rows * BLK * width, bytes_accessed=9 * rows * width, transcendentals=rows * BLK * width // HD
        ),
        name="near",
    )(core, queries, keys, values)


def far_kernel(core_ref, q_ref, kv_ref, acc_ref, stat_ref, *rest, group):
    o_ref = rest[-1]
    pieces, _, _, picks, piece_rows, _ = kv_ref.shape
    far = pieces * picks * piece_rows
    keys = kv_ref[:, 0, 0].reshape(far, HD)
    values = kv_ref[:, 0, 1].reshape(far, HD)
    for g in range(group):
        cols = slice(g * HD, (g + 1) * HD)
        near_top = stat_ref[0, :, 2 * g : 2 * g + 1]
        near_total = stat_ref[0, :, 2 * g + 1 : 2 * g + 2]
        raw = lax.dot_general(q_ref[:, cols], keys, NT, preferred_element_type=jnp.float32)
        top = jnp.maximum(jnp.max(raw, axis=1, keepdims=True), near_top)
        weights = jnp.exp2((raw - top) * EXP_SCALE)
        keep = jnp.exp2((near_top - top) * EXP_SCALE)
        total = jnp.sum(weights, axis=1, keepdims=True) + keep * near_total
        mixed = lax.dot_general(weights.astype(jnp.bfloat16), values, NN, preferred_element_type=jnp.float32)
        mixed = (mixed + keep * acc_ref[:, cols]) / total
        o_ref[:, cols] = mixed.astype(o_ref.dtype)


def far_part(parity, queries, kv, acc, stat, prior):
    rows, width = queries.shape
    pieces, ys, _, picks, piece_rows, _ = kv.shape
    heads = stat.shape[0]
    group = stat.shape[2] // 2
    per = heads // ys
    strip = pl.BlockSpec((rows, group * HD), lambda y, parity: (0, per * y + parity[0]))
    in_specs = [
        strip,
        pl.BlockSpec((pieces, 1, 2, picks, piece_rows, HD), lambda y, parity: (0, y, 0, 0, 0, 0)),
        strip,
        pl.BlockSpec((1, rows, 2 * group), lambda y, parity: (per * y + parity[0], 0, 0)),
    ]
    operands = [parity, queries, kv, acc, stat]
    aliases = {}
    if prior is not None:
        in_specs.append(pl.BlockSpec(memory_space=pl.ANY))
        operands.append(prior)
        aliases = {5: 0}
    far = pieces * picks * piece_rows
    return pl.pallas_call(
        functools.partial(far_kernel, group=group),
        grid_spec=pltpu.PrefetchScalarGridSpec(
            num_scalar_prefetch=1, grid=(ys,), in_specs=in_specs, out_specs=strip
        ),
        out_shape=jax.ShapeDtypeStruct((rows, width), queries.dtype),
        input_output_aliases=aliases,
        cost_estimate=pl.CostEstimate(
            flops=4 * rows * far * width // per,
            bytes_accessed=4 * rows * width + kv.size * 2,
            transcendentals=rows * far * width // HD // per,
        ),
        compiler_params=pltpu.CompilerParams(vmem_limit_bytes=48 * 1024 * 1024),
        name="far",
    )(*operands)


def local(queries, new_keys, new_values, cache_keys, cache_values, chosen):
    ctx_size = lax.axis_size("ctx")
    ys = lax.axis_size("y")
    core = lax.axis_index("core").astype(jnp.int32)
    picks = chosen.shape[2]

    outgoing = spread(cache_keys, cache_values, ctx_size)
    held = lax.all_to_all(outgoing, "ctx", split_axis=0, concat_axis=0, tiled=True)
    ids = lax.all_gather(chosen.reshape(-1), "ctx", tiled=True)

    swap = [(0, 1), (1, 0)]
    mine = jnp.concatenate([new_keys, new_values], axis=1)
    theirs = lax.ppermute(mine, "core", swap)
    both = jnp.where(core == 0, jnp.concatenate([mine, theirs]), jnp.concatenate([theirs, mine]))
    width = new_keys.shape[1]
    acc, stat = near_part(core.reshape(1), queries, both[:, :width], both[:, width:])

    chosen_pieces = pick(ids, held, picks)
    got = lax.all_to_all(chosen_pieces, ("ctx", "y"), split_axis=0, concat_axis=0, tiled=True)
    other = lax.ppermute(got, "core", swap)
    split = (ctx_size, ys) + got.shape[1:]
    out = far_part(core.reshape(1), queries, got.reshape(split), acc, stat, None)
    return far_part((1 - core).reshape(1), queries, other.reshape(split), acc, stat, out)


def solution(mesh):
    ctx_size, head_size = mesh.devices.shape
    fine = Mesh(mesh.devices.reshape(ctx_size, head_size // 2, 2), ("ctx", "y", "core"))
    rows = P(("ctx", "y", "core"), None)
    in_specs = (
        rows,
        rows,
        rows,
        P("ctx", ("y", "core")),
        P("ctx", ("y", "core")),
        P("ctx", ("y", "core"), None),
    )
    return jax.shard_map(local, mesh=fine, in_specs=in_specs, out_specs=rows, check_vma=False)
```

```python
import functools
import math

import jax
import jax.numpy as jnp
from jax import lax
from jax.experimental import pallas as pl
from jax.experimental.pallas import tpu as pltpu
from jax.sharding import Mesh
from jax.sharding import PartitionSpec as P

HD = 128
BLK = 512
MIB = 1024 * 1024
EXP_SCALE = math.log2(math.e) / math.sqrt(HD)
NEG = -1e30
NT = (((1,), (1,)), ((), ()))
NN = (((1,), (0,)), ((), ()))


def in_hbm(x):
    return pltpu.with_memory_space_constraint(x, pltpu.HBM)


def spread_kernel(ids_ref, k_ref, v_ref, o_ref, cache, stage, sems, out_sems):
    blocks, pieces, rows, _ = k_ref.shape
    copies = []
    for b in range(blocks):
        copies.append(pltpu.make_async_copy(k_ref.at[b], cache.at[2 * b], sems.at[2 * b]))
        copies.append(pltpu.make_async_copy(v_ref.at[b], cache.at[2 * b + 1], sems.at[2 * b + 1]))
    for copy in copies:
        copy.start()
    lane = lax.broadcasted_iota(jnp.int32, (rows, HD), 1)
    ids = jnp.zeros((rows, HD), jnp.int32)
    picks, _, ys = ids_ref.shape
    for y in range(ys):
        for j in range(picks):
            ids = jnp.where(lane == y * picks + j, ids_ref[j, 0, y], ids)
    ids = ids.astype(jnp.float32).astype(stage.dtype)
    for m in range(pieces):
        stage[m, 2 * blocks] = ids
    for part in range(2 * blocks):
        copies[part].wait()
        if part < 2 * blocks - 1:
            for m in range(pieces):
                stage[m, part] = cache[part, m]
    outs = []
    step = pieces // out_sems.shape[0]
    for i in range(0, pieces, step):
        for m in range(i, i + step):
            stage[m, 2 * blocks - 1] = cache[2 * blocks - 1, m]
        outs.append(pltpu.make_async_copy(stage.at[i : i + step], o_ref.at[i : i + step], out_sems.at[i // step]))
        outs[-1].start()
    for copy in outs:
        copy.wait()


def spread(cache_keys, cache_values, chosen, pieces):
    blocks = cache_keys.shape[0] // BLK
    rows = BLK // pieces
    shape = (blocks, pieces, rows, HD)
    message = (pieces, 2 * blocks + 1, rows, HD)
    anywhere = pl.BlockSpec(memory_space=pl.ANY)
    return pl.pallas_call(
        spread_kernel,
        in_specs=[pl.BlockSpec(memory_space=pltpu.SMEM), anywhere, anywhere],
        out_specs=anywhere,
        out_shape=jax.ShapeDtypeStruct(message, cache_keys.dtype),
        scratch_shapes=[
            pltpu.VMEM((2 * blocks, pieces, rows, HD), cache_keys.dtype),
            pltpu.VMEM(message, cache_keys.dtype),
            pltpu.SemaphoreType.DMA((2 * blocks,)),
            pltpu.SemaphoreType.DMA((4,)),
        ],
        name="spread",
    )(chosen.transpose(2, 1, 0), *(in_hbm(x.reshape(shape)) for x in (cache_keys, cache_values)))


def pick_kernel(held_ref, o_ref, wide, ids, sem, *, step, ys, picks):
    sources, parts, _, _ = held_ref.shape
    blocks = (parts - 1) // 2
    at = pl.program_id(0)

    @pl.when(at == 0)
    def _():
        wide[...] = held_ref[:, 2 * blocks].astype(jnp.float32)[:, 0, :].astype(jnp.int32)
        copy = pltpu.make_async_copy(wide, ids, sem)
        copy.start()
        copy.wait()

    for i in range(step):
        for y in range(ys):
            for j in range(picks):
                block_id = ids[at * step + i, y * picks + j]
                src = lax.shift_right_logical(block_id, blocks.bit_length() - 1)
                part = 2 * (block_id & (blocks - 1))
                o_ref[i * ys + y, j] = held_ref[src, pl.ds(part, 2)]


def pick(held, ys, picks):
    sources, parts, rows, _ = held.shape
    step = 8
    return pl.pallas_call(
        functools.partial(pick_kernel, step=step, ys=ys, picks=picks),
        grid=(sources // step,),
        in_specs=[pl.BlockSpec(memory_space=pltpu.VMEM)],
        out_specs=pl.BlockSpec((step * ys, picks, 2, rows, HD), lambda i: (i, 0, 0, 0, 0)),
        out_shape=jax.ShapeDtypeStruct((sources * ys, picks, 2, rows, HD), held.dtype),
        scratch_shapes=[
            pltpu.VMEM((sources, HD), jnp.int32),
            pltpu.SMEM((sources, HD), jnp.int32),
            pltpu.SemaphoreType.DMA,
        ],
        compiler_params=pltpu.CompilerParams(vmem_limit_bytes=8 * MIB),
        name="pick",
    )(pltpu.with_memory_space_constraint(held, pltpu.VMEM))


def near_kernel(core_ref, q_ref, k_ref, v_ref, k2_ref, v2_ref, acc_ref, stat_ref, *, group):
    rows = q_ref.shape[0]
    row = lax.broadcasted_iota(jnp.int32, (rows, 2 * rows), 0)
    col = lax.broadcasted_iota(jnp.int32, (rows, 2 * rows), 1)
    seen = jnp.where(col < rows, col, jnp.where(core_ref[0] == 1, -1, 2 * rows)) <= row
    keys = jnp.concatenate([k_ref[...], k2_ref[...]])
    values = jnp.concatenate([v_ref[...], v2_ref[...]])
    for g in range(group):
        cols = slice(g * HD, (g + 1) * HD)
        raw = lax.dot_general(q_ref[:, cols], keys, NT, preferred_element_type=jnp.float32)
        raw = jnp.where(seen, raw, NEG)
        top = jnp.max(raw, axis=1, keepdims=True)
        weights = jnp.exp2((raw - top) * EXP_SCALE)
        total = jnp.sum(weights, axis=1, keepdims=True)
        acc_ref[:, cols] = lax.dot_general(
            weights.astype(jnp.bfloat16), values, NN, preferred_element_type=jnp.float32
        )
        stat_ref[0, :, 2 * g : 2 * g + 1] = top
        stat_ref[0, :, 2 * g + 1 : 2 * g + 2] = total


def near_part(core, queries, keys, values, their_keys, their_values):
    rows, width = queries.shape
    heads = keys.shape[1] // HD
    group = width // (heads * HD)
    head = pl.BlockSpec((rows, HD), lambda h, core: (0, h))
    return pl.pallas_call(
        functools.partial(near_kernel, group=group),
        grid_spec=pltpu.PrefetchScalarGridSpec(
            num_scalar_prefetch=1,
            grid=(heads,),
            in_specs=[pl.BlockSpec((rows, group * HD), lambda h, core: (0, h)), head, head, head, head],
            out_specs=[
                pl.BlockSpec((rows, group * HD), lambda h, core: (0, h)),
                pl.BlockSpec((1, rows, 2 * group), lambda h, core: (h, 0, 0)),
            ],
        ),
        out_shape=[
            jax.ShapeDtypeStruct((rows, width), jnp.float32),
            jax.ShapeDtypeStruct((heads, rows, 2 * group), jnp.float32),
        ],
        cost_estimate=pl.CostEstimate(
            flops=4 * rows * BLK * width, bytes_accessed=9 * rows * width, transcendentals=rows * BLK * width // HD
        ),
        name="near",
    )(core, queries, keys, values, their_keys, their_values)


def far_kernel(parity_ref, q_ref, kv_ref, acc_ref, stat_ref, *rest, group):
    o_ref = rest[-1]
    y = pl.program_id(0)
    pieces, _, picks, _, piece_rows, _ = kv_ref.shape
    far = pieces * picks * piece_rows
    at = y if kv_ref.shape[1] > 1 else 0
    keys = kv_ref[:, at, :, 0].reshape(far, HD)
    values = kv_ref[:, at, :, 1].reshape(far, HD)
    wide = jnp.concatenate([values, jnp.ones_like(values)], axis=1)
    stat = stat_ref[0]

    def columns(g):
        return slice(g * HD, (g + 1) * HD)

    def scores(g):
        return lax.dot_general(q_ref[:, columns(g)], keys, NT, preferred_element_type=jnp.float32)

    def weigh(g):
        return jnp.exp2(scores(g) * EXP_SCALE - stat[:, 2 * g : 2 * g + 1] * EXP_SCALE).astype(jnp.bfloat16)

    worst = jnp.zeros((q_ref.shape[0], 1), jnp.float32)
    ready = weigh(0)
    for g in range(group):
        weights = ready
        if g + 1 < group:
            ready = weigh(g + 1)
        mixed = lax.dot_general(weights, wide, NN, preferred_element_type=jnp.float32)
        total = mixed[:, HD : HD + 1] + stat[:, 2 * g + 1 : 2 * g + 2]
        worst = jnp.maximum(worst, total)
        o_ref[:, g * HD : (g + 1) * HD] = ((mixed[:, :HD] + acc_ref[:, columns(g)]) / total).astype(o_ref.dtype)

    @pl.when(jnp.logical_not(jnp.max(worst) < 2.0**100))
    def _():
        for g in range(group):
            near_top = stat[:, 2 * g : 2 * g + 1]
            raw = scores(g)
            top = jnp.maximum(jnp.max(raw, axis=1, keepdims=True), near_top)
            exact = jnp.exp2((raw - top) * EXP_SCALE)
            keep = jnp.exp2((near_top - top) * EXP_SCALE)
            total = jnp.sum(exact, axis=1, keepdims=True) + keep * stat[:, 2 * g + 1 : 2 * g + 2]
            mixed = lax.dot_general(exact.astype(jnp.bfloat16), values, NN, preferred_element_type=jnp.float32)
            mixed = (mixed + keep * acc_ref[:, columns(g)]) / total
            o_ref[:, g * HD : (g + 1) * HD] = mixed.astype(o_ref.dtype)


def far_part(parity, queries, kv, acc, stat, prior):
    rows, width = queries.shape
    pieces, ys, picks, _, piece_rows, _ = kv.shape
    heads = stat.shape[0]
    group = stat.shape[2] // 2
    per = heads // ys
    strip = pl.BlockSpec((rows, group * HD), lambda y, parity: (0, per * y + parity[0]))
    in_specs = [
        strip,
        pl.BlockSpec(memory_space=pltpu.VMEM),
        strip,
        pl.BlockSpec((1, rows, 2 * group), lambda y, parity: (per * y + parity[0], 0, 0)),
    ]
    queries, acc, stat = in_hbm(queries), in_hbm(acc), in_hbm(stat)
    aliases = {}
    if prior is None:
        operands = [parity, queries, pltpu.with_memory_space_constraint(kv, pltpu.VMEM), acc, stat]
    else:
        in_specs[1] = pl.BlockSpec((pieces, 1, picks, 2, piece_rows, HD), lambda y, parity: (0, y, 0, 0, 0, 0))
        in_specs.append(pl.BlockSpec(memory_space=pl.ANY))
        operands = [parity, queries, in_hbm(kv), acc, stat, prior]
        aliases = {5: 0}
    far = pieces * picks * piece_rows
    return pl.pallas_call(
        functools.partial(far_kernel, group=group),
        grid_spec=pltpu.PrefetchScalarGridSpec(
            num_scalar_prefetch=1,
            grid=(ys,),
            in_specs=in_specs,
            out_specs=strip,
        ),
        out_shape=jax.ShapeDtypeStruct((rows, width), queries.dtype),
        input_output_aliases=aliases,
        cost_estimate=pl.CostEstimate(
            flops=4 * rows * far * width // per,
            bytes_accessed=4 * rows * width + kv.size * 2,
            transcendentals=rows * far * width // HD // per,
        ),
        compiler_params=pltpu.CompilerParams(vmem_limit_bytes=32 * MIB),
        name="far",
    )(*operands)


def local(queries, new_keys, new_values, cache_keys, cache_values, chosen):
    ctx_size = lax.axis_size("ctx")
    ys = lax.axis_size("y")
    core = lax.axis_index("core").astype(jnp.int32)
    picks = chosen.shape[2]

    outgoing = spread(cache_keys, cache_values, chosen, ctx_size)
    held = lax.all_to_all(outgoing, "ctx", split_axis=0, concat_axis=0, tiled=True)

    swap = [(0, 1), (1, 0)]
    their_keys = lax.ppermute(new_keys, "core", swap)
    their_values = lax.ppermute(new_values, "core", swap)
    near = near_part(core.reshape(1), queries, new_keys, new_values, their_keys, their_values)
    held, (acc, stat) = lax.optimization_barrier((held, near))

    got = lax.all_to_all(pick(held, ys, picks), ("ctx", "y"), split_axis=0, concat_axis=0, tiled=True)
    other = lax.ppermute(got, "core", swap)
    split = (ctx_size, ys) + got.shape[1:]
    out = far_part(core.reshape(1), queries, got.reshape(split), acc, stat, None)
    other, out = lax.optimization_barrier((other, out))
    return far_part((1 - core).reshape(1), queries, other.reshape(split), acc, stat, out)


def solution(mesh):
    ctx_size, head_size = mesh.devices.shape
    fine = Mesh(mesh.devices.reshape(ctx_size, head_size // 2, 2), ("ctx", "y", "core"))
    rows = P(("ctx", "y", "core"), None)
    in_specs = (
        rows,
        rows,
        rows,
        P("ctx", ("y", "core")),
        P("ctx", ("y", "core")),
        P("ctx", ("y", "core"), None),
    )
    return jax.shard_map(local, mesh=fine, in_specs=in_specs, out_specs=rows, check_vma=False)
```

```python
import functools
import math

import jax
import jax.numpy as jnp
from jax import lax
from jax.experimental import pallas as pl
from jax.experimental.pallas import tpu as pltpu
from jax.sharding import Mesh
from jax.sharding import PartitionSpec as P

HD = 128
BLK = 512
MIB = 1024 * 1024
EXP_SCALE = math.log2(math.e) / math.sqrt(HD)
NEG = -1e30
NT = (((1,), (1,)), ((), ()))
NN = (((1,), (0,)), ((), ()))


def in_hbm(x):
    return pltpu.with_memory_space_constraint(x, pltpu.HBM)


def spread_kernel(chosen_ref, k_ref, v_ref, o_ref, chosen, cache, stage, sems, out_sems, fetch_sem):
    blocks, pieces, rows, _ = k_ref.shape
    groups = out_sems.shape[0]
    parts = [pl.ds(i * (pieces // groups), pieces // groups) for i in range(groups)]
    copies = [
        [pltpu.make_async_copy(ref.at[:, part], cache.at[at, :, part], sems.at[at, i]) for at, ref in enumerate((k_ref, v_ref))]
        for i, part in enumerate(parts)
    ]
    fetch = pltpu.make_async_copy(chosen_ref, chosen, fetch_sem)
    fetch.start()
    for pair in copies:
        for copy in pair:
            copy.start()
    fetch.wait()
    lane = lax.broadcasted_iota(jnp.int32, (rows, HD), 1)
    ids = jnp.zeros((rows, HD), jnp.int32)
    picks, _, ys = chosen.shape
    for y in range(ys):
        for j in range(picks):
            ids = jnp.where(lane == y * picks + j, chosen[j, 0, y], ids)
    ids = ids.astype(jnp.float32).astype(stage.dtype)
    outs = []
    for i, part in enumerate(parts):
        for copy in copies[i]:
            copy.wait()
        for m in range(part.start, part.start + part.size):
            for b in range(blocks):
                stage[m, 2 * b] = cache[0, b, m]
                stage[m, 2 * b + 1] = cache[1, b, m]
            stage[m, 2 * blocks] = ids
        outs.append(pltpu.make_async_copy(stage.at[part], o_ref.at[part], out_sems.at[i]))
        outs[-1].start()
    for copy in outs:
        copy.wait()


def spread(cache_keys, cache_values, chosen, pieces):
    blocks = cache_keys.shape[0] // BLK
    rows = BLK // pieces
    shape = (blocks, pieces, rows, HD)
    message = (pieces, 2 * blocks + 1, rows, HD)
    anywhere = pl.BlockSpec(memory_space=pl.ANY)
    groups = 4
    return pl.pallas_call(
        spread_kernel,
        in_specs=[anywhere, anywhere, anywhere],
        out_specs=anywhere,
        out_shape=pltpu.HBM(message, cache_keys.dtype),
        scratch_shapes=[
            pltpu.SMEM(chosen.shape[::-1], chosen.dtype),
            pltpu.VMEM((2,) + shape, cache_keys.dtype),
            pltpu.VMEM(message, cache_keys.dtype),
            pltpu.SemaphoreType.DMA((2, groups)),
            pltpu.SemaphoreType.DMA((groups,)),
            pltpu.SemaphoreType.DMA,
        ],
        compiler_params=pltpu.CompilerParams(vmem_limit_bytes=8 * MIB),
        name="spread",
    )(*(in_hbm(x) for x in (chosen.transpose(2, 1, 0), cache_keys.reshape(shape), cache_values.reshape(shape))))


def pick_kernel(held_ref, o_ref, wide, ids, sem, *, step, ys, picks):
    sources, parts, _, _ = held_ref.shape
    blocks = (parts - 1) // 2
    at = pl.program_id(0)

    @pl.when(at == 0)
    def _():
        wide[...] = held_ref[:, 2 * blocks].astype(jnp.float32)[:, 0, :].astype(jnp.int32)
        copy = pltpu.make_async_copy(wide, ids, sem)
        copy.start()
        copy.wait()

    for i in range(step):
        for y in range(ys):
            for j in range(picks):
                block_id = ids[at * step + i, y * picks + j]
                src = lax.shift_right_logical(block_id, blocks.bit_length() - 1)
                part = 2 * (block_id & (blocks - 1))
                o_ref[i * ys + y, j] = held_ref[src, pl.ds(part, 2)]


def pick(held, ys, picks):
    sources, parts, rows, _ = held.shape
    step = 8
    return pl.pallas_call(
        functools.partial(pick_kernel, step=step, ys=ys, picks=picks),
        grid=(sources // step,),
        in_specs=[pl.BlockSpec(memory_space=pltpu.VMEM)],
        out_specs=pl.BlockSpec((step * ys, picks, 2, rows, HD), lambda i: (i, 0, 0, 0, 0)),
        out_shape=jax.ShapeDtypeStruct((sources * ys, picks, 2, rows, HD), held.dtype),
        scratch_shapes=[
            pltpu.VMEM((sources, HD), jnp.int32),
            pltpu.SMEM((sources, HD), jnp.int32),
            pltpu.SemaphoreType.DMA,
        ],
        compiler_params=pltpu.CompilerParams(vmem_limit_bytes=8 * MIB),
        name="pick",
    )(pltpu.with_memory_space_constraint(held, pltpu.VMEM))


def near_kernel(core_ref, q_ref, k_ref, v_ref, k2_ref, v2_ref, acc_ref, stat_ref, *, group):
    rows = q_ref.shape[0]
    key = lax.broadcasted_iota(jnp.int32, (2 * rows, rows), 0)
    query = lax.broadcasted_iota(jnp.int32, (2 * rows, rows), 1)
    seen = jnp.where(key < rows, key, jnp.where(core_ref[0] == 1, -1, 2 * rows)) <= query
    keys = jnp.concatenate([k_ref[...], k2_ref[...]])
    values = jnp.concatenate([v_ref[...], v2_ref[...]]).T
    for g in range(group):
        cols = slice(g * HD, (g + 1) * HD)
        raw = lax.dot_general(keys, q_ref[:, cols], NT, preferred_element_type=jnp.float32)
        raw = jnp.where(seen, raw, NEG)
        top = jnp.max(raw, axis=0, keepdims=True)
        weights = jnp.exp2((raw - top) * EXP_SCALE)
        stat_ref[0, 2 * g : 2 * g + 1] = top
        stat_ref[0, 2 * g + 1 : 2 * g + 2] = jnp.sum(weights, axis=0, keepdims=True)
        acc_ref[0, cols] = lax.dot_general(
            values, weights.astype(jnp.bfloat16), NN, preferred_element_type=jnp.float32
        )


def near_part(core, queries, keys, values, their_keys, their_values):
    rows, width = queries.shape
    heads = keys.shape[1] // HD
    strip = width // heads
    group = strip // HD
    head = pl.BlockSpec((rows, HD), lambda h, core: (0, h))
    return pl.pallas_call(
        functools.partial(near_kernel, group=group),
        grid_spec=pltpu.PrefetchScalarGridSpec(
            num_scalar_prefetch=1,
            grid=(heads,),
            in_specs=[pl.BlockSpec((rows, strip), lambda h, core: (0, h)), head, head, head, head],
            out_specs=[
                pl.BlockSpec((1, strip, rows), lambda h, core: (h, 0, 0)),
                pl.BlockSpec((1, 2 * group, rows), lambda h, core: (h, 0, 0)),
            ],
        ),
        out_shape=[
            pltpu.HBM((heads, strip, rows), jnp.float32),
            pltpu.HBM((heads, 2 * group, rows), jnp.float32),
        ],
        cost_estimate=pl.CostEstimate(
            flops=4 * rows * BLK * width, bytes_accessed=9 * rows * width, transcendentals=rows * BLK * width // HD
        ),
        compiler_params=pltpu.CompilerParams(vmem_limit_bytes=24 * MIB),
        name="near",
    )(core, *(in_hbm(x) for x in (queries, keys, values, their_keys, their_values)))


def far_kernel(parity_ref, q_ref, kv_ref, acc_ref, stat_ref, *rest, group):
    o_ref = rest[-1]
    pieces, _, picks, _, piece_rows, _ = kv_ref.shape
    far = pieces * picks * piece_rows
    at = pl.program_id(0) if kv_ref.shape[1] > 1 else 0
    keys = kv_ref[:, at, :, 0].reshape(far, HD)
    values = kv_ref[:, at, :, 1].reshape(far, HD).T
    tall = jnp.concatenate([values, jnp.ones((16, far), values.dtype)], axis=0)

    def columns(g):
        return slice(g * HD, (g + 1) * HD)

    def near_top(g):
        return stat_ref[0, 2 * g : 2 * g + 1]

    def scores(g):
        return lax.dot_general(keys, q_ref[:, columns(g)], NT, preferred_element_type=jnp.float32)

    def weigh(g):
        return jnp.exp2(scores(g) * EXP_SCALE - near_top(g) * EXP_SCALE).astype(jnp.bfloat16)

    def put(g, weights, keep):
        mixed = lax.dot_general(tall, weights, NN, preferred_element_type=jnp.float32)
        total = mixed[HD : HD + 1] + keep * stat_ref[0, 2 * g + 1 : 2 * g + 2]
        mixed = (mixed[:HD] + keep * acc_ref[0, columns(g)]) / total
        o_ref[:, columns(g)] = mixed.T.astype(o_ref.dtype)
        return total

    worst = 0.0
    ready = weigh(0)
    for g in range(group):
        weights = ready
        if g + 1 < group:
            ready = weigh(g + 1)
        worst = jnp.maximum(worst, put(g, weights, 1.0))

    @pl.when(jnp.logical_not(jnp.max(worst) < 2.0**100))
    def _():
        for g in range(group):
            raw = scores(g)
            top = jnp.maximum(jnp.max(raw, axis=0, keepdims=True), near_top(g))
            exact = jnp.exp2((raw - top) * EXP_SCALE).astype(jnp.bfloat16)
            put(g, exact, jnp.exp2((near_top(g) - top) * EXP_SCALE))


def far_part(parity, queries, kv, acc, stat, prior):
    rows, width = queries.shape
    pieces, ys, picks, _, piece_rows, _ = kv.shape
    heads, strip, _ = acc.shape
    per = heads // ys
    columns = pl.BlockSpec((rows, strip), lambda y, parity: (0, per * y + parity[0]))
    in_specs = [
        columns,
        pl.BlockSpec(memory_space=pltpu.VMEM),
        pl.BlockSpec((1, strip, rows), lambda y, parity: (per * y + parity[0], 0, 0)),
        pl.BlockSpec((1, stat.shape[1], rows), lambda y, parity: (per * y + parity[0], 0, 0)),
    ]
    operands = [parity, in_hbm(queries), pltpu.with_memory_space_constraint(kv, pltpu.VMEM), in_hbm(acc), in_hbm(stat)]
    aliases = {}
    if prior is not None:
        in_specs[1] = pl.BlockSpec((pieces, 1, picks, 2, piece_rows, HD), lambda y, parity: (0, y, 0, 0, 0, 0))
        in_specs.append(pl.BlockSpec(memory_space=pl.ANY))
        operands[2] = in_hbm(kv)
        operands.append(prior)
        aliases = {5: 0}
    far = pieces * picks * piece_rows
    return pl.pallas_call(
        functools.partial(far_kernel, group=strip // HD),
        grid_spec=pltpu.PrefetchScalarGridSpec(
            num_scalar_prefetch=1, grid=(ys,), in_specs=in_specs, out_specs=columns
        ),
        out_shape=jax.ShapeDtypeStruct((rows, width), queries.dtype),
        input_output_aliases=aliases,
        cost_estimate=pl.CostEstimate(
            flops=4 * rows * far * width // per,
            bytes_accessed=4 * rows * width + kv.size * 2,
            transcendentals=rows * far * width // HD // per,
        ),
        compiler_params=pltpu.CompilerParams(vmem_limit_bytes=32 * MIB),
        name="far",
    )(*operands)


def local(queries, new_keys, new_values, cache_keys, cache_values, chosen):
    ctx_size = lax.axis_size("ctx")
    ys = lax.axis_size("y")
    core = lax.axis_index("core").astype(jnp.int32)
    picks = chosen.shape[2]

    outgoing = spread(cache_keys, cache_values, chosen, ctx_size)
    held = lax.all_to_all(outgoing, "ctx", split_axis=0, concat_axis=0, tiled=True)

    swap = [(0, 1), (1, 0)]
    their_keys = lax.ppermute(new_keys, "core", swap)
    their_values = lax.ppermute(new_values, "core", swap)
    near = near_part(core.reshape(1), queries, new_keys, new_values, their_keys, their_values)
    held, (acc, stat) = lax.optimization_barrier((held, near))

    got = lax.all_to_all(pick(held, ys, picks), ("ctx", "y"), split_axis=0, concat_axis=0, tiled=True)
    other = lax.ppermute(got, "core", swap)
    split = (ctx_size, ys) + got.shape[1:]
    out = far_part(core.reshape(1), queries, got.reshape(split), acc, stat, None)
    other, out = lax.optimization_barrier((other, out))
    return far_part((1 - core).reshape(1), queries, other.reshape(split), acc, stat, out)


def solution(mesh):
    ctx_size, head_size = mesh.devices.shape
    fine = Mesh(mesh.devices.reshape(ctx_size, head_size // 2, 2), ("ctx", "y", "core"))
    rows = P(("ctx", "y", "core"), None)
    in_specs = (
        rows,
        rows,
        rows,
        P("ctx", ("y", "core")),
        P("ctx", ("y", "core")),
        P("ctx", ("y", "core"), None),
    )
    return jax.shard_map(local, mesh=fine, in_specs=in_specs, out_specs=rows, check_vma=False)
```

```python
import functools
import math

import jax
import jax.numpy as jnp
from jax import lax
from jax.experimental import pallas as pl
from jax.experimental.pallas import tpu as pltpu
from jax.sharding import Mesh
from jax.sharding import PartitionSpec as P

HD = 128
BLK = 512
MIB = 1024 * 1024
EXP_SCALE = math.log2(math.e) / math.sqrt(HD)
NEG = -1e30
ID_ROWS = 8
NT = (((1,), (1,)), ((), ()))
NN = (((1,), (0,)), ((), ()))


def in_hbm(x):
    return pltpu.with_memory_space_constraint(x, pltpu.HBM)


def spread_kernel(chosen_ref, k_ref, v_ref, o_ref, chosen, cache, stage, sems, out_sems, fetch_sem):
    blocks, pieces, rows, _ = k_ref.shape
    groups = out_sems.shape[0]
    parts = [pl.ds(i * (pieces // groups), pieces // groups) for i in range(groups)]
    copies = [
        [pltpu.make_async_copy(ref.at[:, part], cache.at[at, :, part], sems.at[at, i]) for at, ref in enumerate((k_ref, v_ref))]
        for i, part in enumerate(parts)
    ]
    fetch = pltpu.make_async_copy(chosen_ref, chosen, fetch_sem)
    fetch.start()
    for pair in copies:
        for copy in pair:
            copy.start()
    fetch.wait()
    lane = lax.broadcasted_iota(jnp.int32, (ID_ROWS, HD), 1)
    ids = jnp.zeros((ID_ROWS, HD), jnp.int32)
    picks, _, ys = chosen.shape
    for y in range(ys):
        for j in range(picks):
            ids = jnp.where(lane == y * picks + j, chosen[j, 0, y], ids)
    ids = ids.astype(jnp.float32).astype(stage.dtype)
    outs = []
    for i, part in enumerate(parts):
        for copy in copies[i]:
            copy.wait()
        for m in range(part.start, part.start + part.size):
            for b in range(blocks):
                for at in range(2):
                    stage[m, pl.ds((2 * b + at) * rows, rows)] = cache[at, b, m]
            stage[m, pl.ds(2 * blocks * rows, ID_ROWS)] = ids
        outs.append(pltpu.make_async_copy(stage.at[part], o_ref.at[part], out_sems.at[i]))
        outs[-1].start()
    for copy in outs:
        copy.wait()


def spread(cache_keys, cache_values, chosen, pieces):
    blocks = cache_keys.shape[0] // BLK
    rows = BLK // pieces
    shape = (blocks, pieces, rows, HD)
    message = (pieces, 2 * blocks * rows + ID_ROWS, HD)
    anywhere = pl.BlockSpec(memory_space=pl.ANY)
    groups = 4
    return pl.pallas_call(
        spread_kernel,
        in_specs=[anywhere, anywhere, anywhere],
        out_specs=anywhere,
        out_shape=pltpu.HBM(message, cache_keys.dtype),
        scratch_shapes=[
            pltpu.SMEM(chosen.shape[::-1], chosen.dtype),
            pltpu.VMEM((2,) + shape, cache_keys.dtype),
            pltpu.VMEM(message, cache_keys.dtype),
            pltpu.SemaphoreType.DMA((2, groups)),
            pltpu.SemaphoreType.DMA((groups,)),
            pltpu.SemaphoreType.DMA,
        ],
        compiler_params=pltpu.CompilerParams(vmem_limit_bytes=8 * MIB),
        name="spread",
    )(*(in_hbm(x) for x in (chosen.transpose(2, 1, 0), cache_keys.reshape(shape), cache_values.reshape(shape))))


def pick_kernel(held_ref, o_ref, wide, ids, sem, *, step, ys, picks, blocks, rows):
    at = pl.program_id(0)

    @pl.when(at == 0)
    def _():
        tail = held_ref[:, 2 * blocks * rows :].astype(jnp.float32)
        wide[...] = tail[:, 0, :].astype(jnp.int32)
        copy = pltpu.make_async_copy(wide, ids, sem)
        copy.start()
        copy.wait()

    for i in range(step):
        for y in range(ys):
            for j in range(picks):
                block_id = ids[at * step + i, y * picks + j]
                src = lax.shift_right_logical(block_id, blocks.bit_length() - 1)
                first = pl.multiple_of(2 * rows * (block_id & (blocks - 1)), 2 * rows)
                o_ref[i * ys + y, j] = held_ref[src, pl.ds(first, 2 * rows)].reshape(2, rows, HD)


def pick(held, ys, picks, blocks):
    sources, length, _ = held.shape
    rows = (length - ID_ROWS) // (2 * blocks)
    step = 8
    return pl.pallas_call(
        functools.partial(pick_kernel, step=step, ys=ys, picks=picks, blocks=blocks, rows=rows),
        grid=(sources // step,),
        in_specs=[pl.BlockSpec(memory_space=pltpu.VMEM)],
        out_specs=pl.BlockSpec((step * ys, picks, 2, rows, HD), lambda i: (i, 0, 0, 0, 0)),
        out_shape=jax.ShapeDtypeStruct((sources * ys, picks, 2, rows, HD), held.dtype),
        scratch_shapes=[
            pltpu.VMEM((sources, HD), jnp.int32),
            pltpu.SMEM((sources, HD), jnp.int32),
            pltpu.SemaphoreType.DMA,
        ],
        compiler_params=pltpu.CompilerParams(vmem_limit_bytes=8 * MIB),
        name="pick",
    )(pltpu.with_memory_space_constraint(held, pltpu.VMEM))


def near_kernel(core_ref, q_ref, k_ref, v_ref, k2_ref, v2_ref, acc_ref, stat_ref, *, group):
    rows = q_ref.shape[0]
    key = lax.broadcasted_iota(jnp.int32, (2 * rows, rows), 0)
    query = lax.broadcasted_iota(jnp.int32, (2 * rows, rows), 1)
    seen = jnp.where(key < rows, key, jnp.where(core_ref[0] == 1, -1, 2 * rows)) <= query
    keys = jnp.concatenate([k_ref[...], k2_ref[...]])
    values = jnp.concatenate([v_ref[...], v2_ref[...]]).T
    for g in range(group):
        cols = slice(g * HD, (g + 1) * HD)
        raw = lax.dot_general(keys, q_ref[:, cols], NT, preferred_element_type=jnp.float32)
        raw = jnp.where(seen, raw, NEG)
        top = jnp.max(raw, axis=0, keepdims=True)
        weights = jnp.exp2((raw - top) * EXP_SCALE)
        stat_ref[0, 2 * g : 2 * g + 1] = top
        stat_ref[0, 2 * g + 1 : 2 * g + 2] = jnp.sum(weights, axis=0, keepdims=True)
        acc_ref[0, cols] = lax.dot_general(
            values, weights.astype(jnp.bfloat16), NN, preferred_element_type=jnp.float32
        )


def near_part(core, queries, keys, values, their_keys, their_values):
    rows, width = queries.shape
    heads = keys.shape[1] // HD
    strip = width // heads
    group = strip // HD
    head = pl.BlockSpec((rows, HD), lambda h, core: (0, h))
    return pl.pallas_call(
        functools.partial(near_kernel, group=group),
        grid_spec=pltpu.PrefetchScalarGridSpec(
            num_scalar_prefetch=1,
            grid=(heads,),
            in_specs=[pl.BlockSpec((rows, strip), lambda h, core: (0, h)), head, head, head, head],
            out_specs=[
                pl.BlockSpec((1, strip, rows), lambda h, core: (h, 0, 0)),
                pl.BlockSpec((1, 2 * group, rows), lambda h, core: (h, 0, 0)),
            ],
        ),
        out_shape=[
            pltpu.HBM((heads, strip, rows), jnp.float32),
            pltpu.HBM((heads, 2 * group, rows), jnp.float32),
        ],
        cost_estimate=pl.CostEstimate(
            flops=4 * rows * BLK * width, bytes_accessed=9 * rows * width, transcendentals=rows * BLK * width // HD
        ),
        compiler_params=pltpu.CompilerParams(vmem_limit_bytes=24 * MIB),
        name="near",
    )(core, *(in_hbm(x) for x in (queries, keys, values, their_keys, their_values)))


def far_kernel(parity_ref, q_ref, kv_ref, acc_ref, stat_ref, *rest, group):
    o_ref = rest[-1]
    pieces, _, picks, _, piece_rows, _ = kv_ref.shape
    far = pieces * picks * piece_rows
    at = pl.program_id(0) if kv_ref.shape[1] > 1 else 0
    keys = kv_ref[:, at, :, 0].reshape(far, HD)
    values = kv_ref[:, at, :, 1].reshape(far, HD).T
    tall = jnp.concatenate([values, jnp.ones((16, far), values.dtype)], axis=0)

    def columns(g):
        return slice(g * HD, (g + 1) * HD)

    def near_top(g):
        return stat_ref[0, 2 * g : 2 * g + 1]

    def scores(g):
        return lax.dot_general(keys, q_ref[:, columns(g)], NT, preferred_element_type=jnp.float32)

    def weigh(g):
        return jnp.exp2(scores(g) * EXP_SCALE - near_top(g) * EXP_SCALE).astype(jnp.bfloat16)

    def put(g, weights, keep):
        mixed = lax.dot_general(tall, weights, NN, preferred_element_type=jnp.float32)
        total = mixed[HD : HD + 1] + keep * stat_ref[0, 2 * g + 1 : 2 * g + 2]
        mixed = (mixed[:HD] + keep * acc_ref[0, columns(g)]) / total
        o_ref[:, columns(g)] = mixed.T.astype(o_ref.dtype)
        return total

    worst = 0.0
    ready = weigh(0)
    for g in range(group):
        weights = ready
        if g + 1 < group:
            ready = weigh(g + 1)
        worst = jnp.maximum(worst, put(g, weights, 1.0))

    @pl.when(jnp.logical_not(jnp.max(worst) < 2.0**100))
    def _():
        for g in range(group):
            raw = scores(g)
            top = jnp.maximum(jnp.max(raw, axis=0, keepdims=True), near_top(g))
            exact = jnp.exp2((raw - top) * EXP_SCALE).astype(jnp.bfloat16)
            put(g, exact, jnp.exp2((near_top(g) - top) * EXP_SCALE))


def far_part(parity, queries, kv, acc, stat, prior):
    rows, width = queries.shape
    pieces, ys, picks, _, piece_rows, _ = kv.shape
    heads, strip, _ = acc.shape
    per = heads // ys
    columns = pl.BlockSpec((rows, strip), lambda y, parity: (0, per * y + parity[0]))
    in_specs = [
        columns,
        pl.BlockSpec(memory_space=pltpu.VMEM),
        pl.BlockSpec((1, strip, rows), lambda y, parity: (per * y + parity[0], 0, 0)),
        pl.BlockSpec((1, stat.shape[1], rows), lambda y, parity: (per * y + parity[0], 0, 0)),
    ]
    operands = [parity, in_hbm(queries), pltpu.with_memory_space_constraint(kv, pltpu.VMEM), in_hbm(acc), in_hbm(stat)]
    aliases = {}
    if prior is not None:
        in_specs[1] = pl.BlockSpec((pieces, 1, picks, 2, piece_rows, HD), lambda y, parity: (0, y, 0, 0, 0, 0))
        in_specs.append(pl.BlockSpec(memory_space=pl.ANY))
        operands[2] = in_hbm(kv)
        operands.append(prior)
        aliases = {5: 0}
    far = pieces * picks * piece_rows
    return pl.pallas_call(
        functools.partial(far_kernel, group=strip // HD),
        grid_spec=pltpu.PrefetchScalarGridSpec(
            num_scalar_prefetch=1, grid=(ys,), in_specs=in_specs, out_specs=columns
        ),
        out_shape=jax.ShapeDtypeStruct((rows, width), queries.dtype),
        input_output_aliases=aliases,
        cost_estimate=pl.CostEstimate(
            flops=4 * rows * far * width // per,
            bytes_accessed=4 * rows * width + kv.size * 2,
            transcendentals=rows * far * width // HD // per,
        ),
        compiler_params=pltpu.CompilerParams(vmem_limit_bytes=32 * MIB),
        name="far",
    )(*operands)


def local(queries, new_keys, new_values, cache_keys, cache_values, chosen):
    ctx_size = lax.axis_size("ctx")
    ys = lax.axis_size("y")
    core = lax.axis_index("core").astype(jnp.int32)
    picks = chosen.shape[2]

    outgoing = spread(cache_keys, cache_values, chosen, ctx_size)
    held = lax.all_to_all(outgoing, "ctx", split_axis=0, concat_axis=0, tiled=True)

    swap = [(0, 1), (1, 0)]
    their_keys = lax.ppermute(new_keys, "core", swap)
    their_values = lax.ppermute(new_values, "core", swap)
    near = near_part(core.reshape(1), queries, new_keys, new_values, their_keys, their_values)
    held, (acc, stat) = lax.optimization_barrier((held, near))

    got = lax.all_to_all(pick(held, ys, picks, cache_keys.shape[0] // BLK), ("ctx", "y"), split_axis=0, concat_axis=0, tiled=True)
    other = lax.ppermute(got, "core", swap)
    split = (ctx_size, ys) + got.shape[1:]
    out = far_part(core.reshape(1), queries, got.reshape(split), acc, stat, None)
    other, out = lax.optimization_barrier((other, out))
    return far_part((1 - core).reshape(1), queries, other.reshape(split), acc, stat, out)


def solution(mesh):
    ctx_size, head_size = mesh.devices.shape
    fine = Mesh(mesh.devices.reshape(ctx_size, head_size // 2, 2), ("ctx", "y", "core"))
    rows = P(("ctx", "y", "core"), None)
    in_specs = (
        rows,
        rows,
        rows,
        P("ctx", ("y", "core")),
        P("ctx", ("y", "core")),
        P("ctx", ("y", "core"), None),
    )
    return jax.shard_map(local, mesh=fine, in_specs=in_specs, out_specs=rows, check_vma=False)
```

```python
import functools
import math

import jax
import jax.numpy as jnp
from jax import lax
from jax.experimental import pallas as pl
from jax.experimental.pallas import tpu as pltpu
from jax.sharding import Mesh
from jax.sharding import PartitionSpec as P

HD = 128
BLK = 512
MIB = 1024 * 1024
EXP_SCALE = math.log2(math.e) / math.sqrt(HD)
NEG = -1e30
ID_ROWS = 8
FAR_HEADS = 2
NT = (((1,), (1,)), ((), ()))
NN = (((1,), (0,)), ((), ()))


def in_hbm(x):
    return pltpu.with_memory_space_constraint(x, pltpu.HBM)


def spread_kernel(chosen_ref, k_ref, v_ref, o_ref, chosen, cache, stage, sems, out_sems, fetch_sem):
    blocks, pieces, rows, _ = k_ref.shape
    groups = out_sems.shape[0]
    parts = [pl.ds(i * (pieces // groups), pieces // groups) for i in range(groups)]
    copies = [
        [pltpu.make_async_copy(ref.at[:, part], cache.at[at, :, part], sems.at[at, i]) for at, ref in enumerate((k_ref, v_ref))]
        for i, part in enumerate(parts)
    ]
    fetch = pltpu.make_async_copy(chosen_ref, chosen, fetch_sem)
    fetch.start()
    for pair in copies:
        for copy in pair:
            copy.start()
    fetch.wait()
    lane = lax.broadcasted_iota(jnp.int32, (ID_ROWS, HD), 1)
    ids = jnp.zeros((ID_ROWS, HD), jnp.int32)
    picks, _, ys = chosen.shape
    for y in range(ys):
        for j in range(picks):
            ids = jnp.where(lane == y * picks + j, chosen[j, 0, y], ids)
    ids = ids.astype(jnp.float32).astype(stage.dtype)
    outs = []
    for i, part in enumerate(parts):
        for copy in copies[i]:
            copy.wait()
        for m in range(part.start, part.start + part.size):
            for b in range(blocks):
                for at in range(2):
                    stage[m, pl.ds((2 * b + at) * rows, rows)] = cache[at, b, m]
            stage[m, pl.ds(2 * blocks * rows, ID_ROWS)] = ids
        outs.append(pltpu.make_async_copy(stage.at[part], o_ref.at[part], out_sems.at[i]))
        outs[-1].start()
    for copy in outs:
        copy.wait()


def spread(cache_keys, cache_values, chosen, pieces):
    blocks = cache_keys.shape[0] // BLK
    rows = BLK // pieces
    shape = (blocks, pieces, rows, HD)
    message = (pieces, 2 * blocks * rows + ID_ROWS, HD)
    anywhere = pl.BlockSpec(memory_space=pl.ANY)
    groups = 4
    return pl.pallas_call(
        spread_kernel,
        in_specs=[anywhere, anywhere, anywhere],
        out_specs=anywhere,
        out_shape=pltpu.HBM(message, cache_keys.dtype),
        scratch_shapes=[
            pltpu.SMEM(chosen.shape[::-1], chosen.dtype),
            pltpu.VMEM((2,) + shape, cache_keys.dtype),
            pltpu.VMEM(message, cache_keys.dtype),
            pltpu.SemaphoreType.DMA((2, groups)),
            pltpu.SemaphoreType.DMA((groups,)),
            pltpu.SemaphoreType.DMA,
        ],
        compiler_params=pltpu.CompilerParams(vmem_limit_bytes=8 * MIB),
        name="spread",
    )(*(in_hbm(x) for x in (chosen.transpose(2, 1, 0), cache_keys.reshape(shape), cache_values.reshape(shape))))


def pick_kernel(held_ref, o_ref, wide, ids, sem, *, ys, picks, blocks, rows):
    tail = held_ref[:, 2 * blocks * rows :].astype(jnp.float32)
    wide[...] = tail[:, 0, :].astype(jnp.int32)
    copy = pltpu.make_async_copy(wide, ids, sem)
    copy.start()
    copy.wait()

    def one(at, carry):
        for y in range(ys):
            for j in range(picks):
                block_id = ids[at, y * picks + j]
                src = lax.shift_right_logical(block_id, blocks.bit_length() - 1)
                first = pl.multiple_of(2 * rows * (block_id & (blocks - 1)), 2 * rows)
                o_ref[at * ys + y, j] = held_ref[src, pl.ds(first, 2 * rows)].reshape(2, rows, HD)
        return carry

    lax.fori_loop(0, held_ref.shape[0], one, 0, unroll=4)


def pick(held, ys, picks, blocks):
    sources, length, _ = held.shape
    rows = (length - ID_ROWS) // (2 * blocks)
    return pl.pallas_call(
        functools.partial(pick_kernel, ys=ys, picks=picks, blocks=blocks, rows=rows),
        in_specs=[pl.BlockSpec(memory_space=pltpu.VMEM)],
        out_specs=pl.BlockSpec(memory_space=pltpu.VMEM),
        out_shape=pltpu.VMEM((sources * ys, picks, 2, rows, HD), held.dtype),
        scratch_shapes=[
            pltpu.VMEM((sources, HD), jnp.int32),
            pltpu.SMEM((sources, HD), jnp.int32),
            pltpu.SemaphoreType.DMA,
        ],
        compiler_params=pltpu.CompilerParams(vmem_limit_bytes=8 * MIB),
        name="pick",
    )(pltpu.with_memory_space_constraint(held, pltpu.VMEM))


def near_kernel(core_ref, q_ref, k_ref, v_ref, k2_ref, v2_ref, acc_ref, stat_ref, *, group):
    rows = q_ref.shape[0]
    key = lax.broadcasted_iota(jnp.int32, (2 * rows, rows), 0)
    query = lax.broadcasted_iota(jnp.int32, (2 * rows, rows), 1)
    seen = jnp.where(key < rows, key, jnp.where(core_ref[0] == 1, -1, 2 * rows)) <= query
    keys = jnp.concatenate([k_ref[...], k2_ref[...]])
    values = jnp.concatenate([v_ref[...], v2_ref[...]]).T
    for g in range(group):
        cols = slice(g * HD, (g + 1) * HD)
        raw = lax.dot_general(keys, q_ref[:, cols], NT, preferred_element_type=jnp.float32)
        raw = jnp.where(seen, raw, NEG)
        top = jnp.max(raw, axis=0, keepdims=True)
        weights = jnp.exp2((raw - top) * EXP_SCALE)
        stat_ref[0, 2 * g : 2 * g + 1] = top
        stat_ref[0, 2 * g + 1 : 2 * g + 2] = jnp.sum(weights, axis=0, keepdims=True)
        acc_ref[0, cols] = lax.dot_general(
            values, weights.astype(jnp.bfloat16), NN, preferred_element_type=jnp.float32
        )


def near_part(core, queries, keys, values, their_keys, their_values):
    rows, width = queries.shape
    heads = keys.shape[1] // HD
    strip = width // heads
    group = strip // HD
    head = pl.BlockSpec((rows, HD), lambda h, core: (0, h))
    return pl.pallas_call(
        functools.partial(near_kernel, group=group),
        grid_spec=pltpu.PrefetchScalarGridSpec(
            num_scalar_prefetch=1,
            grid=(heads,),
            in_specs=[pl.BlockSpec((rows, strip), lambda h, core: (0, h)), head, head, head, head],
            out_specs=[
                pl.BlockSpec((1, strip, rows), lambda h, core: (h, 0, 0)),
                pl.BlockSpec((1, 2 * group, rows), lambda h, core: (h, 0, 0)),
            ],
        ),
        out_shape=[
            pltpu.HBM((heads, strip, rows), jnp.float32),
            pltpu.HBM((heads, 2 * group, rows), jnp.float32),
        ],
        cost_estimate=pl.CostEstimate(
            flops=4 * rows * BLK * width, bytes_accessed=9 * rows * width, transcendentals=rows * BLK * width // HD
        ),
        compiler_params=pltpu.CompilerParams(vmem_limit_bytes=24 * MIB),
        name="near",
    )(core, *(in_hbm(x) for x in (queries, keys, values, their_keys, their_values)))


def far_kernel(parity_ref, *refs, heads, group, per, ys):
    q_refs, (kv_ref, acc_ref, stat_ref, *_, o_hbm, done, sems) = refs[:heads], refs[heads:]
    step = pl.program_id(0)
    pieces, _, picks, _, piece_rows, _ = kv_ref.shape
    far = pieces * picks * piece_rows
    keys, tall = [], []
    for k in range(heads):
        at = step * heads + k if kv_ref.shape[1] > heads else k
        keys.append(kv_ref[:, at, :, 0].reshape(far, HD))
        values = kv_ref[:, at, :, 1].reshape(far, HD).T
        tall.append(jnp.concatenate([values, jnp.ones((16, far), values.dtype)], axis=0))
    items = [(k, g) for k in range(heads) for g in range(group)]

    def columns(g):
        return slice(g * HD, (g + 1) * HD)

    def near_top(k, g):
        return stat_ref[k, 0, 2 * g : 2 * g + 1]

    def scores(k, g):
        return lax.dot_general(keys[k], q_refs[k][:, columns(g)], NT, preferred_element_type=jnp.float32)

    def weigh(k, g):
        return jnp.exp2(scores(k, g) * EXP_SCALE - near_top(k, g) * EXP_SCALE).astype(jnp.bfloat16)

    def put(k, g, weights, keep):
        mixed = lax.dot_general(tall[k], weights, NN, preferred_element_type=jnp.float32)
        total = mixed[HD : HD + 1] + keep * stat_ref[k, 0, 2 * g + 1 : 2 * g + 2]
        mixed = (mixed[:HD] + keep * acc_ref[k, 0, columns(g)]) / total
        done[step * heads + k, :, columns(g)] = mixed.T.astype(done.dtype)
        return total

    worst = 0.0
    ready = weigh(*items[0])
    for at, item in enumerate(items):
        weights = ready
        if at + 1 < len(items):
            ready = weigh(*items[at + 1])
        worst = jnp.maximum(worst, put(*item, weights, 1.0))

    @pl.when(jnp.logical_not(jnp.max(worst) < 2.0**100))
    def _():
        for item in items:
            raw = scores(*item)
            top = jnp.maximum(jnp.max(raw, axis=0, keepdims=True), near_top(*item))
            exact = jnp.exp2((raw - top) * EXP_SCALE).astype(jnp.bfloat16)
            put(*item, exact, jnp.exp2((near_top(*item) - top) * EXP_SCALE))

    def out_copy(y):
        strip = pl.ds(pl.multiple_of((per * y + parity_ref[0]) * group * HD, group * HD), group * HD)
        return pltpu.make_async_copy(done.at[y], o_hbm.at[:, strip], sems.at[y])

    for k in range(heads):
        out_copy(step * heads + k).start()

    @pl.when(step == ys // heads - 1)
    def _():
        for y in range(ys):
            out_copy(y).wait()


def far_part(parity, queries, kv, acc, stat, prior):
    rows, width = queries.shape
    pieces, ys, picks, _, piece_rows, _ = kv.shape
    strip = acc.shape[1]
    per = acc.shape[0] // ys
    heads = FAR_HEADS
    anywhere = pl.BlockSpec(memory_space=pl.ANY)

    def column(k):
        return pl.BlockSpec((rows, strip), lambda i, parity: (0, per * (i * heads + k) + parity[0]))

    def by_head(x):
        x = x.reshape((ys, per) + x.shape[1:])
        return pl.BlockSpec((heads, 1) + x.shape[2:], lambda i, parity: (i, parity[0], 0, 0)), in_hbm(x)

    (acc_spec, acc), (stat_spec, stat) = by_head(acc), by_head(stat)
    if prior is None:
        kv_spec, kv = pl.BlockSpec(memory_space=pltpu.VMEM), pltpu.with_memory_space_constraint(kv, pltpu.VMEM)
    else:
        kv_spec = pl.BlockSpec((pieces, heads, picks, 2, piece_rows, HD), lambda i, parity: (0, i, 0, 0, 0, 0))
        kv = in_hbm(kv)
    in_specs = [column(k) for k in range(heads)] + [kv_spec, acc_spec, stat_spec]
    operands = [parity] + [in_hbm(queries)] * heads + [kv, acc, stat]
    aliases = {}
    if prior is not None:
        in_specs.append(anywhere)
        aliases = {len(operands): 0}
        operands.append(prior)
    far = pieces * picks * piece_rows
    return pl.pallas_call(
        functools.partial(far_kernel, heads=heads, group=strip // HD, per=per, ys=ys),
        grid_spec=pltpu.PrefetchScalarGridSpec(
            num_scalar_prefetch=1,
            grid=(ys // heads,),
            in_specs=in_specs,
            out_specs=anywhere,
            scratch_shapes=[pltpu.VMEM((ys, rows, strip), queries.dtype), pltpu.SemaphoreType.DMA((ys,))],
        ),
        out_shape=jax.ShapeDtypeStruct((rows, width), queries.dtype),
        input_output_aliases=aliases,
        cost_estimate=pl.CostEstimate(
            flops=4 * rows * far * width // per,
            bytes_accessed=4 * rows * width + kv.size * 2,
            transcendentals=rows * far * width // HD // per,
        ),
        compiler_params=pltpu.CompilerParams(vmem_limit_bytes=40 * MIB),
        name="far",
    )(*operands)


def local(queries, new_keys, new_values, cache_keys, cache_values, chosen):
    ctx_size = lax.axis_size("ctx")
    ys = lax.axis_size("y")
    core = lax.axis_index("core").astype(jnp.int32)
    picks = chosen.shape[2]

    outgoing = spread(cache_keys, cache_values, chosen, ctx_size)
    held = lax.all_to_all(outgoing, "ctx", split_axis=0, concat_axis=0, tiled=True)

    swap = [(0, 1), (1, 0)]
    their_keys = lax.ppermute(new_keys, "core", swap)
    their_values = lax.ppermute(new_values, "core", swap)
    near = near_part(core.reshape(1), queries, new_keys, new_values, their_keys, their_values)
    held, (acc, stat) = lax.optimization_barrier((held, near))

    got = lax.all_to_all(pick(held, ys, picks, cache_keys.shape[0] // BLK), ("ctx", "y"), split_axis=0, concat_axis=0, tiled=True)
    other = lax.ppermute(got, "core", swap)
    split = (ctx_size, ys) + got.shape[1:]
    out = far_part(core.reshape(1), queries, got.reshape(split), acc, stat, None)
    other, out = lax.optimization_barrier((other, out))
    return far_part((1 - core).reshape(1), queries, other.reshape(split), acc, stat, out)


def solution(mesh):
    ctx_size, head_size = mesh.devices.shape
    fine = Mesh(mesh.devices.reshape(ctx_size, head_size // 2, 2), ("ctx", "y", "core"))
    rows = P(("ctx", "y", "core"), None)
    in_specs = (
        rows,
        rows,
        rows,
        P("ctx", ("y", "core")),
        P("ctx", ("y", "core")),
        P("ctx", ("y", "core"), None),
    )
    return jax.shard_map(local, mesh=fine, in_specs=in_specs, out_specs=rows, check_vma=False)
```

```python
import functools
import math

import jax
import jax.numpy as jnp
from jax import lax
from jax.experimental import pallas as pl
from jax.experimental.pallas import tpu as pltpu
from jax.sharding import Mesh
from jax.sharding import PartitionSpec as P

HD = 128
BLK = 512
MIB = 1024 * 1024
EXP_SCALE = math.log2(math.e) / math.sqrt(HD)
NEG = -1e30
ID_ROWS = 8
FAR_HEADS = 2
NT = (((1,), (1,)), ((), ()))
NN = (((1,), (0,)), ((), ()))


def in_hbm(x):
    return pltpu.with_memory_space_constraint(x, pltpu.HBM)


def spread_kernel(chosen_ref, k_ref, v_ref, o_ref, chosen, cache, stage, sems, out_sems, fetch_sem):
    blocks, pieces, rows, _ = k_ref.shape
    groups = out_sems.shape[0]
    parts = [pl.ds(i * (pieces // groups), pieces // groups) for i in range(groups)]
    copies = [
        [pltpu.make_async_copy(ref.at[:, part], cache.at[at, :, part], sems.at[at, i]) for at, ref in enumerate((k_ref, v_ref))]
        for i, part in enumerate(parts)
    ]
    fetch = pltpu.make_async_copy(chosen_ref, chosen, fetch_sem)
    fetch.start()
    for pair in copies:
        for copy in pair:
            copy.start()
    fetch.wait()
    lane = lax.broadcasted_iota(jnp.int32, (ID_ROWS, HD), 1)
    ids = jnp.zeros((ID_ROWS, HD), jnp.int32)
    picks, _, ys = chosen.shape
    for y in range(ys):
        for j in range(picks):
            ids = jnp.where(lane == y * picks + j, chosen[j, 0, y], ids)
    ids = ids.astype(jnp.float32).astype(stage.dtype)
    outs = []
    for i, part in enumerate(parts):
        for copy in copies[i]:
            copy.wait()
        for m in range(part.start, part.start + part.size):
            for b in range(blocks):
                for at in range(2):
                    stage[m, pl.ds((2 * b + at) * rows, rows)] = cache[at, b, m]
            stage[m, pl.ds(2 * blocks * rows, ID_ROWS)] = ids
        outs.append(pltpu.make_async_copy(stage.at[part], o_ref.at[part], out_sems.at[i]))
        outs[-1].start()
    for copy in outs:
        copy.wait()


def spread(cache_keys, cache_values, chosen, pieces):
    blocks = cache_keys.shape[0] // BLK
    rows = BLK // pieces
    shape = (blocks, pieces, rows, HD)
    message = (pieces, 2 * blocks * rows + ID_ROWS, HD)
    anywhere = pl.BlockSpec(memory_space=pl.ANY)
    groups = 4
    return pl.pallas_call(
        spread_kernel,
        in_specs=[anywhere, anywhere, anywhere],
        out_specs=anywhere,
        out_shape=pltpu.HBM(message, cache_keys.dtype),
        scratch_shapes=[
            pltpu.SMEM(chosen.shape[::-1], chosen.dtype),
            pltpu.VMEM((2,) + shape, cache_keys.dtype),
            pltpu.VMEM(message, cache_keys.dtype),
            pltpu.SemaphoreType.DMA((2, groups)),
            pltpu.SemaphoreType.DMA((groups,)),
            pltpu.SemaphoreType.DMA,
        ],
        compiler_params=pltpu.CompilerParams(vmem_limit_bytes=8 * MIB),
        name="spread",
    )(*(in_hbm(x) for x in (chosen.transpose(2, 1, 0), cache_keys.reshape(shape), cache_values.reshape(shape))))


def pick_kernel(held_ref, o_ref, wide, ids, sem, *, ys, picks, blocks, rows):
    tail = held_ref[:, 2 * blocks * rows :].astype(jnp.float32)
    wide[...] = tail[:, 0, :].astype(jnp.int32)
    copy = pltpu.make_async_copy(wide, ids, sem)
    copy.start()
    copy.wait()

    def one(at, carry):
        for y in range(ys):
            for j in range(picks):
                block_id = ids[at, y * picks + j]
                src = lax.shift_right_logical(block_id, blocks.bit_length() - 1)
                first = pl.multiple_of(2 * rows * (block_id & (blocks - 1)), 2 * rows)
                o_ref[y, at, j] = held_ref[src, pl.ds(first, 2 * rows)].reshape(2, rows, HD)
        return carry

    lax.fori_loop(0, held_ref.shape[0], one, 0, unroll=8)


def pick(held, ys, picks, blocks):
    sources, length, _ = held.shape
    rows = (length - ID_ROWS) // (2 * blocks)
    return pl.pallas_call(
        functools.partial(pick_kernel, ys=ys, picks=picks, blocks=blocks, rows=rows),
        in_specs=[pl.BlockSpec(memory_space=pltpu.VMEM)],
        out_specs=pl.BlockSpec(memory_space=pltpu.VMEM),
        out_shape=pltpu.VMEM((ys, sources, picks, 2, rows, HD), held.dtype),
        scratch_shapes=[
            pltpu.VMEM((sources, HD), jnp.int32),
            pltpu.SMEM((sources, HD), jnp.int32),
            pltpu.SemaphoreType.DMA,
        ],
        compiler_params=pltpu.CompilerParams(vmem_limit_bytes=8 * MIB),
        name="pick",
    )(pltpu.with_memory_space_constraint(held, pltpu.VMEM))


def near_kernel(core_ref, q_ref, k_ref, v_ref, k2_ref, v2_ref, acc_ref, stat_ref, *, group):
    rows = q_ref.shape[0]
    key = lax.broadcasted_iota(jnp.int32, (2 * rows, rows), 0)
    query = lax.broadcasted_iota(jnp.int32, (2 * rows, rows), 1)
    seen = jnp.where(key < rows, key, jnp.where(core_ref[0] == 1, -1, 2 * rows)) <= query
    keys = jnp.concatenate([k_ref[...], k2_ref[...]])
    values = jnp.concatenate([v_ref[...], v2_ref[...]]).T
    for g in range(group):
        cols = slice(g * HD, (g + 1) * HD)
        raw = lax.dot_general(keys, q_ref[:, cols], NT, preferred_element_type=jnp.float32)
        raw = jnp.where(seen, raw, NEG)
        top = jnp.max(raw, axis=0, keepdims=True)
        weights = jnp.exp2((raw - top) * EXP_SCALE)
        stat_ref[0, 2 * g : 2 * g + 1] = top
        stat_ref[0, 2 * g + 1 : 2 * g + 2] = jnp.sum(weights, axis=0, keepdims=True)
        acc_ref[0, cols] = lax.dot_general(
            values, weights.astype(jnp.bfloat16), NN, preferred_element_type=jnp.float32
        )


def near_part(core, queries, keys, values, their_keys, their_values):
    rows, width = queries.shape
    heads = keys.shape[1] // HD
    strip = width // heads
    group = strip // HD
    head = pl.BlockSpec((rows, HD), lambda h, core: (0, h))
    return pl.pallas_call(
        functools.partial(near_kernel, group=group),
        grid_spec=pltpu.PrefetchScalarGridSpec(
            num_scalar_prefetch=1,
            grid=(heads,),
            in_specs=[pl.BlockSpec((rows, strip), lambda h, core: (0, h)), head, head, head, head],
            out_specs=[
                pl.BlockSpec((1, strip, rows), lambda h, core: (h, 0, 0)),
                pl.BlockSpec((1, 2 * group, rows), lambda h, core: (h, 0, 0)),
            ],
        ),
        out_shape=[
            pltpu.HBM((heads, strip, rows), jnp.float32),
            pltpu.HBM((heads, 2 * group, rows), jnp.float32),
        ],
        cost_estimate=pl.CostEstimate(
            flops=4 * rows * BLK * width, bytes_accessed=9 * rows * width, transcendentals=rows * BLK * width // HD
        ),
        compiler_params=pltpu.CompilerParams(vmem_limit_bytes=24 * MIB),
        name="near",
    )(core, *(in_hbm(x) for x in (queries, keys, values, their_keys, their_values)))


def far_kernel(parity_ref, *refs, heads, group, per, ys):
    q_refs, (kv_ref, acc_ref, stat_ref, *_, o_hbm, done, sems) = refs[:heads], refs[heads:]
    step = pl.program_id(0)
    _, pieces, picks, _, piece_rows, _ = kv_ref.shape
    far = pieces * picks * piece_rows
    keys, tall = [], []
    for k in range(heads):
        at = step * heads + k if kv_ref.shape[0] > heads else k
        keys.append(kv_ref[at, :, :, 0].reshape(far, HD))
        values = kv_ref[at, :, :, 1].reshape(far, HD).T
        tall.append(jnp.concatenate([values, jnp.ones((16, far), values.dtype)], axis=0))
    items = [(k, g) for k in range(heads) for g in range(group)]

    def columns(g):
        return slice(g * HD, (g + 1) * HD)

    def near_top(k, g):
        return stat_ref[k, 0, 2 * g : 2 * g + 1]

    def scores(k, g):
        return lax.dot_general(keys[k], q_refs[k][:, columns(g)], NT, preferred_element_type=jnp.float32)

    def weigh(k, g):
        return jnp.exp2(scores(k, g) * EXP_SCALE - near_top(k, g) * EXP_SCALE).astype(jnp.bfloat16)

    def put(k, g, weights, keep):
        mixed = lax.dot_general(tall[k], weights, NN, preferred_element_type=jnp.float32)
        total = mixed[HD : HD + 1] + keep * stat_ref[k, 0, 2 * g + 1 : 2 * g + 2]
        mixed = (mixed[:HD] + keep * acc_ref[k, 0, columns(g)]) / total
        done[step * heads + k, :, columns(g)] = mixed.T.astype(done.dtype)
        return total

    worst = 0.0
    ready = weigh(*items[0])
    for at, item in enumerate(items):
        weights = ready
        if at + 1 < len(items):
            ready = weigh(*items[at + 1])
        worst = jnp.maximum(worst, put(*item, weights, 1.0))

    @pl.when(jnp.logical_not(jnp.max(worst) < 2.0**100))
    def _():
        for item in items:
            raw = scores(*item)
            top = jnp.maximum(jnp.max(raw, axis=0, keepdims=True), near_top(*item))
            exact = jnp.exp2((raw - top) * EXP_SCALE).astype(jnp.bfloat16)
            put(*item, exact, jnp.exp2((near_top(*item) - top) * EXP_SCALE))

    def out_copy(y):
        strip = pl.ds(pl.multiple_of((per * y + parity_ref[0]) * group * HD, group * HD), group * HD)
        return pltpu.make_async_copy(done.at[y], o_hbm.at[:, strip], sems.at[y])

    for k in range(heads):
        out_copy(step * heads + k).start()

    @pl.when(step == ys // heads - 1)
    def _():
        for y in range(ys):
            out_copy(y).wait()


def far_part(parity, queries, kv, acc, stat, prior):
    rows, width = queries.shape
    ys, pieces, picks, _, piece_rows, _ = kv.shape
    strip = acc.shape[1]
    per = acc.shape[0] // ys
    heads = FAR_HEADS
    anywhere = pl.BlockSpec(memory_space=pl.ANY)
    place = in_hbm if prior is None else (lambda x: x)

    def column(k):
        return pl.BlockSpec((rows, strip), lambda i, parity: (0, per * (i * heads + k) + parity[0]))

    def by_head(x):
        x = x.reshape((ys, per) + x.shape[1:])
        return pl.BlockSpec((heads, 1) + x.shape[2:], lambda i, parity: (i, parity[0], 0, 0)), place(x)

    (acc_spec, acc), (stat_spec, stat) = by_head(acc), by_head(stat)
    if prior is None:
        kv_spec, kv = pl.BlockSpec(memory_space=pltpu.VMEM), pltpu.with_memory_space_constraint(kv, pltpu.VMEM)
    else:
        kv_spec = pl.BlockSpec((heads, pieces, picks, 2, piece_rows, HD), lambda i, parity: (i, 0, 0, 0, 0, 0))
        kv = in_hbm(kv)
    in_specs = [column(k) for k in range(heads)] + [kv_spec, acc_spec, stat_spec]
    operands = [parity] + [place(queries)] * heads + [kv, acc, stat]
    aliases = {}
    if prior is not None:
        in_specs.append(anywhere)
        aliases = {len(operands): 0}
        operands.append(prior)
    far = pieces * picks * piece_rows
    return pl.pallas_call(
        functools.partial(far_kernel, heads=heads, group=strip // HD, per=per, ys=ys),
        grid_spec=pltpu.PrefetchScalarGridSpec(
            num_scalar_prefetch=1,
            grid=(ys // heads,),
            in_specs=in_specs,
            out_specs=anywhere,
            scratch_shapes=[pltpu.VMEM((ys, rows, strip), queries.dtype), pltpu.SemaphoreType.DMA((ys,))],
        ),
        out_shape=jax.ShapeDtypeStruct((rows, width), queries.dtype),
        input_output_aliases=aliases,
        cost_estimate=pl.CostEstimate(
            flops=4 * rows * far * width // per,
            bytes_accessed=4 * rows * width + kv.size * 2,
            transcendentals=rows * far * width // HD // per,
        ),
        compiler_params=pltpu.CompilerParams(vmem_limit_bytes=40 * MIB),
        name="far",
    )(*operands)


def local(queries, new_keys, new_values, cache_keys, cache_values, chosen):
    ctx_size = lax.axis_size("ctx")
    ys = lax.axis_size("y")
    core = lax.axis_index("core").astype(jnp.int32)
    picks = chosen.shape[2]

    outgoing = spread(cache_keys, cache_values, chosen, ctx_size)
    held = lax.all_to_all(outgoing, "ctx", split_axis=0, concat_axis=0, tiled=True)

    swap = [(0, 1), (1, 0)]
    their_keys = lax.ppermute(new_keys, "core", swap)
    their_values = lax.ppermute(new_values, "core", swap)
    near = near_part(core.reshape(1), queries, new_keys, new_values, their_keys, their_values)
    held, (acc, stat) = lax.optimization_barrier((held, near))

    chosen_pieces = pick(held, ys, picks, cache_keys.shape[0] // BLK)
    split = chosen_pieces.shape
    chosen_pieces = chosen_pieces.reshape((ys * ctx_size,) + split[2:])
    got = lax.all_to_all(chosen_pieces, ("y", "ctx"), split_axis=0, concat_axis=0, tiled=True)
    other = lax.ppermute(got, "core", swap)
    out = far_part(core.reshape(1), queries, got.reshape(split), acc, stat, None)
    other, out = lax.optimization_barrier((other, out))
    return far_part((1 - core).reshape(1), queries, other.reshape(split), acc, stat, out)


def solution(mesh):
    ctx_size, head_size = mesh.devices.shape
    fine = Mesh(mesh.devices.reshape(ctx_size, head_size // 2, 2), ("ctx", "y", "core"))
    rows = P(("ctx", "y", "core"), None)
    in_specs = (
        rows,
        rows,
        rows,
        P("ctx", ("y", "core")),
        P("ctx", ("y", "core")),
        P("ctx", ("y", "core"), None),
    )
    return jax.shard_map(local, mesh=fine, in_specs=in_specs, out_specs=rows, check_vma=False)
```

```python
import functools
import math

import jax
import jax.numpy as jnp
from jax import lax
from jax.experimental import pallas as pl
from jax.experimental.pallas import tpu as pltpu
from jax.sharding import Mesh
from jax.sharding import PartitionSpec as P

HD = 128
BLK = 512
MIB = 1024 * 1024
EXP_SCALE = math.log2(math.e) / math.sqrt(HD)
NEG = -1e30
ID_ROWS = 8
FAR_HEADS = 2
NT = (((1,), (1,)), ((), ()))
NN = (((1,), (0,)), ((), ()))


def in_hbm(x):
    return pltpu.with_memory_space_constraint(x, pltpu.HBM)


def spread_kernel(chosen_ref, k_ref, v_ref, o_ref, chosen, cache, stage, sems, out_sems, fetch_sem):
    blocks, pieces, rows, _ = k_ref.shape
    groups = out_sems.shape[0]
    parts = [pl.ds(i * (pieces // groups), pieces // groups) for i in range(groups)]
    copies = [
        [pltpu.make_async_copy(ref.at[:, part], cache.at[at, :, part], sems.at[at, i]) for at, ref in enumerate((k_ref, v_ref))]
        for i, part in enumerate(parts)
    ]
    fetch = pltpu.make_async_copy(chosen_ref, chosen, fetch_sem)
    fetch.start()
    for pair in copies:
        for copy in pair:
            copy.start()
    fetch.wait()
    lane = lax.broadcasted_iota(jnp.int32, (ID_ROWS, HD), 1)
    ids = jnp.zeros((ID_ROWS, HD), jnp.int32)
    picks, _, ys = chosen.shape
    for y in range(ys):
        for j in range(picks):
            ids = jnp.where(lane == y * picks + j, chosen[j, 0, y], ids)
    ids = ids.astype(jnp.float32).astype(stage.dtype)
    outs = []
    for i, part in enumerate(parts):
        for copy in copies[i]:
            copy.wait()
        for m in range(part.start, part.start + part.size):
            for b in range(blocks):
                for at in range(2):
                    stage[m, pl.ds((2 * b + at) * rows, rows)] = cache[at, b, m]
            stage[m, pl.ds(2 * blocks * rows, ID_ROWS)] = ids
        outs.append(pltpu.make_async_copy(stage.at[part], o_ref.at[part], out_sems.at[i]))
        outs[-1].start()
    for copy in outs:
        copy.wait()


def spread(cache_keys, cache_values, chosen, pieces):
    blocks = cache_keys.shape[0] // BLK
    rows = BLK // pieces
    shape = (blocks, pieces, rows, HD)
    message = (pieces, 2 * blocks * rows + ID_ROWS, HD)
    anywhere = pl.BlockSpec(memory_space=pl.ANY)
    groups = 4
    return pl.pallas_call(
        spread_kernel,
        in_specs=[anywhere, anywhere, anywhere],
        out_specs=anywhere,
        out_shape=pltpu.HBM(message, cache_keys.dtype),
        scratch_shapes=[
            pltpu.SMEM(chosen.shape[::-1], chosen.dtype),
            pltpu.VMEM((2,) + shape, cache_keys.dtype),
            pltpu.VMEM(message, cache_keys.dtype),
            pltpu.SemaphoreType.DMA((2, groups)),
            pltpu.SemaphoreType.DMA((groups,)),
            pltpu.SemaphoreType.DMA,
        ],
        compiler_params=pltpu.CompilerParams(vmem_limit_bytes=8 * MIB),
        name="spread",
    )(*(in_hbm(x) for x in (chosen.transpose(2, 1, 0), cache_keys.reshape(shape), cache_values.reshape(shape))))


def pick_kernel(held_ref, o_ref, wide, ids, sem, *, ys, picks, blocks, rows):
    tail = held_ref[:, 2 * blocks * rows :].astype(jnp.float32)
    wide[...] = tail[:, 0, :].astype(jnp.int32)
    copy = pltpu.make_async_copy(wide, ids, sem)
    copy.start()
    copy.wait()

    def one(at, carry):
        for y in range(ys):
            for j in range(picks):
                block_id = ids[at, y * picks + j]
                src = lax.shift_right_logical(block_id, blocks.bit_length() - 1)
                first = pl.multiple_of(2 * rows * (block_id & (blocks - 1)), 2 * rows)
                o_ref[y, at, j] = held_ref[src, pl.ds(first, 2 * rows)].reshape(2, rows, HD)
        return carry

    lax.fori_loop(0, held_ref.shape[0], one, 0, unroll=8)


def pick(held, ys, picks, blocks):
    sources, length, _ = held.shape
    rows = (length - ID_ROWS) // (2 * blocks)
    return pl.pallas_call(
        functools.partial(pick_kernel, ys=ys, picks=picks, blocks=blocks, rows=rows),
        in_specs=[pl.BlockSpec(memory_space=pltpu.VMEM)],
        out_specs=pl.BlockSpec(memory_space=pltpu.VMEM),
        out_shape=pltpu.VMEM((ys, sources, picks, 2, rows, HD), held.dtype),
        scratch_shapes=[
            pltpu.VMEM((sources, HD), jnp.int32),
            pltpu.SMEM((sources, HD), jnp.int32),
            pltpu.SemaphoreType.DMA,
        ],
        compiler_params=pltpu.CompilerParams(vmem_limit_bytes=8 * MIB),
        name="pick",
    )(pltpu.with_memory_space_constraint(held, pltpu.VMEM))


def near_kernel(core_ref, q_ref, k_ref, v_ref, k2_ref, v2_ref, acc_ref, stat_ref, *, group):
    rows = q_ref.shape[0]
    key = lax.broadcasted_iota(jnp.int32, (2 * rows, rows), 0)
    query = lax.broadcasted_iota(jnp.int32, (2 * rows, rows), 1)
    seen = jnp.where(key < rows, key, jnp.where(core_ref[0] == 1, -1, 2 * rows)) <= query
    keys = jnp.concatenate([k_ref[...], k2_ref[...]])
    values = jnp.concatenate([v_ref[...], v2_ref[...]]).T
    for g in range(group):
        cols = slice(g * HD, (g + 1) * HD)
        raw = lax.dot_general(keys, q_ref[:, cols], NT, preferred_element_type=jnp.float32)
        raw = jnp.where(seen, raw, NEG)
        top = jnp.max(raw, axis=0, keepdims=True)
        weights = jnp.exp2((raw - top) * EXP_SCALE)
        stat_ref[0, 2 * g : 2 * g + 1] = top
        stat_ref[0, 2 * g + 1 : 2 * g + 2] = jnp.sum(weights, axis=0, keepdims=True)
        acc_ref[0, cols] = lax.dot_general(
            values, weights.astype(jnp.bfloat16), NN, preferred_element_type=jnp.float32
        ).astype(acc_ref.dtype)


def near_part(core, queries, keys, values, their_keys, their_values):
    rows, width = queries.shape
    heads = keys.shape[1] // HD
    strip = width // heads
    group = strip // HD
    head = pl.BlockSpec((rows, HD), lambda h, core: (0, h))
    return pl.pallas_call(
        functools.partial(near_kernel, group=group),
        grid_spec=pltpu.PrefetchScalarGridSpec(
            num_scalar_prefetch=1,
            grid=(heads,),
            in_specs=[pl.BlockSpec((rows, strip), lambda h, core: (0, h)), head, head, head, head],
            out_specs=[
                pl.BlockSpec((1, strip, rows), lambda h, core: (h, 0, 0)),
                pl.BlockSpec((1, 2 * group, rows), lambda h, core: (h, 0, 0)),
            ],
        ),
        out_shape=[
            pltpu.HBM((heads, strip, rows), jnp.bfloat16),
            pltpu.HBM((heads, 2 * group, rows), jnp.float32),
        ],
        cost_estimate=pl.CostEstimate(
            flops=4 * rows * BLK * width, bytes_accessed=9 * rows * width, transcendentals=rows * BLK * width // HD
        ),
        compiler_params=pltpu.CompilerParams(vmem_limit_bytes=24 * MIB),
        name="near",
    )(core, *(in_hbm(x) for x in (queries, keys, values, their_keys, their_values)))


def far_kernel(parity_ref, *refs, heads, group, per, ys):
    q_refs, (kv_ref, acc_ref, stat_ref, *_, o_hbm, done, sems) = refs[:heads], refs[heads:]
    step = pl.program_id(0)
    _, pieces, picks, _, piece_rows, _ = kv_ref.shape
    far = pieces * picks * piece_rows
    keys, tall = [], []
    for k in range(heads):
        at = step * heads + k if kv_ref.shape[0] > heads else k
        keys.append(kv_ref[at, :, :, 0].reshape(far, HD))
        values = kv_ref[at, :, :, 1].reshape(far, HD).T
        tall.append(jnp.concatenate([values, jnp.ones((16, far), values.dtype)], axis=0))
    items = [(k, g) for k in range(heads) for g in range(group)]

    def columns(g):
        return slice(g * HD, (g + 1) * HD)

    def near_top(k, g):
        return stat_ref[k, 0, 2 * g : 2 * g + 1]

    def scores(k, g):
        return lax.dot_general(keys[k], q_refs[k][:, columns(g)], NT, preferred_element_type=jnp.float32)

    def weigh(k, g):
        return jnp.exp2(scores(k, g) * EXP_SCALE - near_top(k, g) * EXP_SCALE).astype(jnp.bfloat16)

    def put(k, g, weights, keep):
        mixed = lax.dot_general(tall[k], weights, NN, preferred_element_type=jnp.float32)
        total = mixed[HD : HD + 1] + keep * stat_ref[k, 0, 2 * g + 1 : 2 * g + 2]
        mixed = (mixed[:HD] + keep * acc_ref[k, 0, columns(g)].astype(jnp.float32)) / total
        done[step * heads + k, :, columns(g)] = mixed.T.astype(done.dtype)
        return total

    worst = 0.0
    ready = weigh(*items[0])
    for at, item in enumerate(items):
        weights = ready
        if at + 1 < len(items):
            ready = weigh(*items[at + 1])
        worst = jnp.maximum(worst, put(*item, weights, 1.0))

    @pl.when(jnp.logical_not(jnp.max(worst) < 2.0**100))
    def _():
        for item in items:
            raw = scores(*item)
            top = jnp.maximum(jnp.max(raw, axis=0, keepdims=True), near_top(*item))
            exact = jnp.exp2((raw - top) * EXP_SCALE).astype(jnp.bfloat16)
            put(*item, exact, jnp.exp2((near_top(*item) - top) * EXP_SCALE))

    def out_copy(y):
        strip = pl.ds(pl.multiple_of((per * y + parity_ref[0]) * group * HD, group * HD), group * HD)
        return pltpu.make_async_copy(done.at[y], o_hbm.at[:, strip], sems.at[y])

    for k in range(heads):
        out_copy(step * heads + k).start()

    @pl.when(step == ys // heads - 1)
    def _():
        for y in range(ys):
            out_copy(y).wait()


def far_part(parity, queries, kv, acc, stat, prior):
    rows, width = queries.shape
    ys, pieces, picks, _, piece_rows, _ = kv.shape
    strip = acc.shape[1]
    per = acc.shape[0] // ys
    heads = FAR_HEADS
    anywhere = pl.BlockSpec(memory_space=pl.ANY)
    place = in_hbm if prior is None else (lambda x: x)

    def column(k):
        return pl.BlockSpec((rows, strip), lambda i, parity: (0, per * (i * heads + k) + parity[0]))

    def by_head(x):
        x = x.reshape((ys, per) + x.shape[1:])
        return pl.BlockSpec((heads, 1) + x.shape[2:], lambda i, parity: (i, parity[0], 0, 0)), place(x)

    (acc_spec, acc), (stat_spec, stat) = by_head(acc), by_head(stat)
    if prior is None:
        kv_spec, kv = pl.BlockSpec(memory_space=pltpu.VMEM), pltpu.with_memory_space_constraint(kv, pltpu.VMEM)
    else:
        kv_spec = pl.BlockSpec((heads, pieces, picks, 2, piece_rows, HD), lambda i, parity: (i, 0, 0, 0, 0, 0))
        kv = in_hbm(kv)
    in_specs = [column(k) for k in range(heads)] + [kv_spec, acc_spec, stat_spec]
    operands = [parity] + [place(queries)] * heads + [kv, acc, stat]
    aliases = {}
    if prior is not None:
        in_specs.append(anywhere)
        aliases = {len(operands): 0}
        operands.append(prior)
    far = pieces * picks * piece_rows
    return pl.pallas_call(
        functools.partial(far_kernel, heads=heads, group=strip // HD, per=per, ys=ys),
        grid_spec=pltpu.PrefetchScalarGridSpec(
            num_scalar_prefetch=1,
            grid=(ys // heads,),
            in_specs=in_specs,
            out_specs=anywhere,
            scratch_shapes=[pltpu.VMEM((ys, rows, strip), queries.dtype), pltpu.SemaphoreType.DMA((ys,))],
        ),
        out_shape=jax.ShapeDtypeStruct((rows, width), queries.dtype),
        input_output_aliases=aliases,
        cost_estimate=pl.CostEstimate(
            flops=4 * rows * far * width // per,
            bytes_accessed=4 * rows * width + kv.size * 2,
            transcendentals=rows * far * width // HD // per,
        ),
        compiler_params=pltpu.CompilerParams(vmem_limit_bytes=40 * MIB),
        name="far",
    )(*operands)


def local(queries, new_keys, new_values, cache_keys, cache_values, chosen):
    ctx_size = lax.axis_size("ctx")
    ys = lax.axis_size("y")
    core = lax.axis_index("core").astype(jnp.int32)
    picks = chosen.shape[2]

    outgoing = spread(cache_keys, cache_values, chosen, ctx_size)
    held = lax.all_to_all(outgoing, "ctx", split_axis=0, concat_axis=0, tiled=True)

    swap = [(0, 1), (1, 0)]
    their_keys = lax.ppermute(new_keys, "core", swap)
    their_values = lax.ppermute(new_values, "core", swap)
    near = near_part(core.reshape(1), queries, new_keys, new_values, their_keys, their_values)
    held, (acc, stat) = lax.optimization_barrier((held, near))

    chosen_pieces = pick(held, ys, picks, cache_keys.shape[0] // BLK)
    split = chosen_pieces.shape
    chosen_pieces = chosen_pieces.reshape((ys * ctx_size,) + split[2:])
    got = lax.all_to_all(chosen_pieces, ("y", "ctx"), split_axis=0, concat_axis=0, tiled=True)
    other = lax.ppermute(got, "core", swap)
    out = far_part(core.reshape(1), queries, got.reshape(split), acc, stat, None)
    other, out = lax.optimization_barrier((other, out))
    return far_part((1 - core).reshape(1), queries, other.reshape(split), acc, stat, out)


def solution(mesh):
    ctx_size, head_size = mesh.devices.shape
    fine = Mesh(mesh.devices.reshape(ctx_size, head_size // 2, 2), ("ctx", "y", "core"))
    rows = P(("ctx", "y", "core"), None)
    in_specs = (
        rows,
        rows,
        rows,
        P("ctx", ("y", "core")),
        P("ctx", ("y", "core")),
        P("ctx", ("y", "core"), None),
    )
    return jax.shard_map(local, mesh=fine, in_specs=in_specs, out_specs=rows, check_vma=False)
```
